512 devices in a mesh: leaf: 512 (over x, z, y, core).
Axes of the slice: x: 4, y: 4, z: 16, core: 2. Of those that a mesh axis runs over, the one named last changes fastest.
Arguments:
- rhs: float32 [262144, 512], P('leaf'), may hold values from -6 to 6
- leaf_inverse: float32 [262144, 512], P('leaf'), may hold values from -0.25 to 0.25
- basis: float32 [262144, 576], P('leaf'), may hold values from -0.25 to 0.25
- caps: float32 [512, 9, 128, 128], P('leaf'), as said below
Outputs:
- solution: float32 [262144, 512], P('leaf')
The draws below stay inside these ranges and needn't reach their ends.
Inputs may be any that keep to these rules, and one draw needn't show every extreme that they name: caps[d, l] is equal for all leaves d with the same d // 2 ** (l + 1).
All inputs are finite; a program needn't handle non-finite values.
Results may differ from the reference program's by a relative error of at most 0.00014.
Values sent between devices are 32-bit elements; how exact they have to be, the bound alone decides.
No kernel may reach another device: no remote copies, remote signals or barrier semaphores. Data moves between devices by JAX's collectives and lax.ppermute only.
A program may use at most 64 MiB of HBM per device.

```python
import jax
import jax.numpy as jnp
from jax import lax

LEAF = 512
NRHS = 512
RANK = 64
LEVELS = 9
ORDER = 262144
N_LEAF = 512


def draw_caps(key, part):
    key = jax.random.fold_in(key, 7)
    shape = (N_LEAF, LEVELS, 2 * RANK, 2 * RANK)
    raw = jnp.clip(jax.random.normal(key, shape, jnp.float32), -4.0, 4.0)
    level_ids = jnp.arange(LEVELS, dtype=jnp.int32)
    device_ids = jnp.arange(N_LEAF, dtype=jnp.int32)
    node_ids = device_ids[:, None] >> level_ids[None, :] + 1
    picked = raw[node_ids, jnp.broadcast_to(level_ids[None, :], (N_LEAF, LEVELS))]
    scales = (2.0 * RANK) ** (-0.5) * jnp.exp2(-0.5 * (level_ids.astype(jnp.float32) + 1.0))
    return (picked * scales[None, :, None, None]).astype(jnp.float32)


def steps_of(rng, dims, pieces, least, largest):
    loudness = 1.0
    for axis_at, blocks in pieces:
        steps = jax.random.uniform(jax.random.fold_in(jax.random.fold_in(rng, 6), axis_at), (blocks,), jnp.float32, least / len(pieces), largest / len(pieces))
        loudness = loudness * jnp.repeat(jnp.exp(steps), dims[axis_at] // blocks).reshape((-1,) + (1,) * (len(dims) - 1 - axis_at))
    return loudness


def scatter_about(key, dims, scale, bound, shards=(), held_as=jnp.bfloat16):
    array = scale * jax.random.normal(key, dims, jnp.float32)
    if shards:
        array = array * steps_of(key, dims, shards, -0.22, 0.18)
    return jnp.clip(array, -bound, bound).astype(held_as)


def setup_inputs(seed: int = 0) -> dict:
    key_of = jax.random.split(jax.random.key(seed), 5)
    return {
        "rhs": scatter_about(key_of[0], (ORDER, NRHS), 1.0, 6.0, ((0, 512),), jnp.float32),
        "leaf_inverse": scatter_about(key_of[1], (ORDER, LEAF), LEAF ** -0.5, 0.25, ((0, 512),), jnp.float32),
        "basis": scatter_about(key_of[2], (ORDER, LEVELS * RANK), LEAF ** -0.5, 0.25, ((0, 512),), jnp.float32),
        "caps": draw_caps(jax.random.fold_in(key_of[4], 71), 0),
    }


HIGH = lax.Precision.HIGHEST


def reference(rhs, leaf_inverse, basis, caps):
    blocks = rhs.reshape(N_LEAF, LEAF, NRHS)
    inverses = leaf_inverse.reshape(N_LEAF, LEAF, LEAF)
    iterate = jnp.einsum("dij,djr->dir", inverses, blocks, precision=HIGH)
    factors = basis.reshape(N_LEAF, LEAF, LEVELS, RANK)
    device_ids = jnp.arange(N_LEAF, dtype=jnp.int32)
    for level_index in range(LEVELS):
        level_basis = factors[:, :, level_index, :]
        local_term = jnp.einsum("dik,dir->dkr", level_basis, iterate, precision=HIGH)
        half_size = 2 ** level_index
        group_sums = local_term.reshape(N_LEAF // half_size, half_size, RANK, NRHS).sum(axis=1)
        pair_sums = group_sums.reshape(N_LEAF // (2 * half_size), 2 * RANK, NRHS)
        coupled = jnp.repeat(pair_sums, 2 * half_size, axis=0)
        applied = jnp.einsum("dab,dbr->dar", caps[:, level_index], coupled, precision=HIGH)
        half_bit = ((device_ids >> level_index) & 1)[:, None, None]
        correction = jnp.where(half_bit == 0, applied[:, :RANK], applied[:, RANK:])
        iterate = iterate - jnp.einsum("dik,dkr->dir", level_basis, correction, precision=HIGH)
    return iterate.reshape(N_LEAF * LEAF, NRHS)
```

```python
import jax
import jax.numpy as jnp
from jax import lax
from jax.sharding import PartitionSpec as P

HIGH = lax.Precision.HIGH
HIGHEST = lax.Precision.HIGHEST

RANK = 64
LEVELS = 9
PARTNER = (1, 2, 6, 8, 16, 32, 96, 128, 384)


def aligned(size, count):
    return [list(range(start, start + size)) for start in range(0, count, size)]


def dot(a, b, dims, precision):
    return lax.dot_general(a, b, ((dims[0], dims[1]), ((), ())), precision=precision,
                           preferred_element_type=jnp.float32)


def sent(array, mask):
    count = lax.axis_size("leaf")
    return lax.ppermute(array, "leaf", [(i, i ^ mask) for i in range(count)])


def step(own, other, gram_own, gram_other, cap):
    keep = own.shape[1] - RANK
    pair = jnp.concatenate([own[:, keep:], other[:, keep:]], axis=1)
    both = dot(pair, cap, ((1,), (1,)), HIGHEST)
    if keep == 0:
        return both, None
    gram = jnp.concatenate([gram_own, gram_other], axis=0)
    rest = own[:, :keep] + other[:, :keep] - dot(both, gram, ((1,), (0,)), HIGHEST)
    return both, rest


def local(rhs, leaf_inverse, basis, caps):
    count = lax.axis_size("leaf")
    position = lax.axis_index("leaf")
    bit = [position >> n & 1 for n in range(LEVELS)]
    core, y_low, y_high = bit[0], bit[1], bit[2]
    z_quarter = position >> 5 & 3
    z_half = position >> 6 & 1

    factors = basis.T
    factors = jnp.concatenate(
        [factors[l * RANK : (l + 1) * RANK] for l in range(LEVELS - 1, -1, -1)], axis=0
    )
    gram = dot(factors, factors, ((1,), (1,)), HIGH)

    def gram_row(level):
        top = (LEVELS - 1 - level) * RANK
        return gram[top : top + RANK, :top]

    row2 = gram_row(2)
    octet_part = jnp.concatenate(
        [jnp.where(y_high == 0, row2, 0.0), jnp.where(y_high == 1, row2, 0.0), gram[256:384, :384]],
        axis=0,
    )
    octet_sum = lax.psum(octet_part, "leaf", axis_index_groups=aligned(8, count))
    row5, row6, row7 = gram_row(5), gram_row(6), gram_row(7)
    slots5 = jnp.concatenate([jnp.where(z_quarter == s, row5, 0.0) for s in range(4)], axis=0)
    side7 = jnp.concatenate([row7, jnp.zeros((3 * RANK, RANK), jnp.float32)], axis=0)
    slots6 = jnp.concatenate([jnp.where(z_half == s, row6, 0.0) for s in range(2)], axis=1)
    plane_part = jnp.concatenate([jnp.concatenate([slots5, side7], axis=1), slots6], axis=0)
    plane_sum = lax.psum(plane_part, "leaf", axis_index_groups=aligned(128, count))

    turned = jnp.roll(caps[0], (RANK, RANK), (1, 2))
    half_bits = jnp.stack(bit)[:, None, None]
    caps_own = jnp.where(half_bits == 0, caps[0], turned)

    iterate = dot(leaf_inverse, rhs, ((1,), (0,)), HIGH)
    terms = dot(iterate, factors, ((0,), (1,)), HIGH)

    mine = lax.dynamic_slice_in_dim(terms, core * 256, 256, 0)
    theirs = lax.dynamic_slice_in_dim(terms, (1 - core) * 256, 256, 0)
    low = gram[448:576, :512]
    got = sent(
        jnp.concatenate([theirs, jnp.pad(low, ((0, 0), (0, RANK)))], axis=0), PARTNER[0]
    )
    low_got = got[256:, :512]
    both0, state = step(mine, got[:256], low[64:], low_got[64:], caps_own[0])
    gram1 = low[:64, :448] + low_got[:64, :448]

    part = y_low ^ y_high
    mine = lax.dynamic_slice_in_dim(state, part * 128, 128, 0)
    theirs = lax.dynamic_slice_in_dim(state, (1 - part) * 128, 128, 0)
    got = sent(jnp.concatenate([theirs, jnp.pad(gram1, ((0, 0), (0, RANK)))], axis=0), PARTNER[1])
    both1, state = step(mine, got[:128], gram1, got[128:, :448], caps_own[1])

    mine = lax.dynamic_slice_in_dim(state, y_high * 64, 64, 0)
    theirs = lax.dynamic_slice_in_dim(state, (1 - y_high) * 64, 64, 0)
    got = sent(theirs, PARTNER[2])
    lower2, upper2 = octet_sum[:64, :384], octet_sum[64:128, :384]
    own2 = jnp.where(y_high == 0, lower2, upper2)
    other2 = jnp.where(y_high == 0, upper2, lower2)
    both2, state = step(mine, got, own2, other2, caps_own[2])

    low_gathered = lax.all_gather(
        jnp.concatenate([both0, both1, both2], axis=0), "leaf", axis_index_groups=aligned(8, count)
    )

    gram3, gram4 = octet_sum[192:256, :320], octet_sum[128:192, :256]
    got = sent(jnp.concatenate([state, gram4, gram3], axis=1), PARTNER[3])
    both3, state = step(state, got[:, :384], gram3, got[:, 640:], caps_own[3])
    gram4 = gram4 + got[:, 384:640]

    got = sent(jnp.concatenate([gram4, state], axis=1), PARTNER[4])
    both4, state = step(state, got[:, 256:], gram4, got[:, :256], caps_own[4])

    got = sent(state, PARTNER[5])
    own5 = lax.dynamic_slice_in_dim(plane_sum, z_quarter * 64, 64, 0)[:, :192]
    other5 = lax.dynamic_slice_in_dim(plane_sum, (z_quarter ^ 1) * 64, 64, 0)[:, :192]
    both5, state = step(state, got, own5, other5, caps_own[5])

    got = sent(state, PARTNER[6])
    lower6, upper6 = plane_sum[256:, :128], plane_sum[256:, 128:]
    own6 = jnp.where(z_half == 0, lower6, upper6)
    other6 = jnp.where(z_half == 0, upper6, lower6)
    both6, state = step(state, got, own6, other6, caps_own[6])

    middle_gathered = lax.all_gather(
        jnp.concatenate([both6[:, :64], both5[:, :64], both4[:, :64], both3[:, :64]], axis=1),
        "leaf", axis_index_groups=aligned(8, count),
    )

    gram7 = plane_sum[:64, 192:]
    got = sent(jnp.concatenate([state, gram7], axis=1), PARTNER[7])
    both7, state = step(state, got[:, :128], gram7, got[:, 128:], caps_own[7])

    got = sent(state, PARTNER[8])
    both8, _ = step(state, got, None, None, caps_own[8])

    high_gathered = lax.all_gather(
        jnp.concatenate([both8[:, :64], both7[:, :64]], axis=1),
        "leaf", axis_index_groups=aligned(8, count),
    )

    def place(shard):
        c, b1, b2 = shard >> 2, shard >> 1 & 1, shard & 1
        return b2 << 2 | (b1 ^ b2) << 1 | c

    in_order = [place(s) for s in range(8)]
    octet_place = position & 7
    mine0 = both0[:, :64]
    partner0 = lax.dynamic_index_in_dim(low_gathered, octet_place ^ 1, 0, False)[:256, 64:]
    corr0 = jnp.where(
        core == 0,
        jnp.concatenate([mine0, partner0], axis=0),
        jnp.concatenate([partner0, mine0], axis=0),
    )
    pieces = []
    for c in range(2):
        for b1 in range(2):
            low_bit = b1 ^ y_high
            block = lax.dynamic_index_in_dim(
                low_gathered, y_high << 2 | low_bit << 1 | c, 0, False
            )[256:384]
            pieces.append(jnp.where(low_bit == y_low, block[:, :64], block[:, 64:]))
    corr1 = jnp.concatenate(pieces, axis=0)
    pieces = []
    for s in range(8):
        block = low_gathered[in_order[s], 384:]
        pieces.append(jnp.where(y_high == (s & 1), block[:, :64], block[:, 64:]))
    corr2 = jnp.concatenate(pieces, axis=0)
    middle = jnp.concatenate([middle_gathered[q] for q in in_order], axis=0)
    first = jnp.concatenate([middle, corr2, corr1, corr0], axis=1)
    iterate = iterate - dot(factors[128:], first, ((0,), (1,)), HIGH)
    last = jnp.concatenate([high_gathered[q] for q in in_order], axis=0)
    return iterate - dot(factors[:128], last, ((0,), (1,)), HIGH)


def solution(mesh):
    return jax.shard_map(
        local,
        mesh=mesh,
        in_specs=(P("leaf", None), P("leaf", None), P("leaf", None), P("leaf", None, None, None)),
        out_specs=P("leaf", None),
        check_vma=False,
    )
```

```python
import functools

import jax
import jax.numpy as jnp
from jax import lax
from jax.experimental import pallas as pl
from jax.experimental.pallas import tpu as pltpu
from jax.sharding import PartitionSpec as P

HIGHEST = lax.Precision.HIGHEST
F32 = jnp.float32
BF16 = jnp.bfloat16
RANK = 64
LEVELS = 9
PARTNER = (1, 2, 6, 8, 16, 32, 96, 128, 384)
NN, NT = ((1,), (0,)), ((1,), (1,))
SLAB_FIRST = (3, 3, 3, 4, 4, 5, 5, 6)
SLAB_SECOND = (3, 3, 7, 4, 4, 5, 5, 6)


def bits():
    d = lax.axis_index("leaf")
    core, y_low, y_high = d & 1, d >> 1 & 1, d >> 2 & 1
    return d, core, y_low ^ y_high, y_high


def sent(array, mask):
    count = lax.axis_size("leaf")
    return lax.ppermute(array, "leaf", [(i, i ^ mask) for i in range(count)])


def call(body, outs, *args, flops=0):
    vmem = pl.BlockSpec(memory_space=pltpu.VMEM)
    shapes = [jax.ShapeDtypeStruct(o[0], o[1]) if isinstance(o[0], tuple) else
              jax.ShapeDtypeStruct(o, F32) for o in outs]
    moved = sum(a.size * a.dtype.itemsize for a in args)
    return pl.pallas_call(
        body,
        out_shape=shapes,
        in_specs=[vmem] * len(args),
        out_specs=[vmem] * len(outs),
        compiler_params=pltpu.CompilerParams(vmem_limit_bytes=40 * 2**20),
        cost_estimate=pl.CostEstimate(flops=flops, bytes_accessed=moved, transcendentals=0),
    )(*args)


def mm(a, b, dims):
    return lax.dot_general(a, b, (dims, ((), ())), preferred_element_type=F32)


def split(x):
    high = x.astype(BF16)
    return high, (x - high.astype(F32)).astype(BF16)


def mm3(a, b, dims):
    return mm(a[0], b[0], dims) + (mm(a[0], b[1], dims) + mm(a[1], b[0], dims))


def small(a, b, dims):
    return lax.dot_general(a, b, (dims, ((), ())), precision=HIGHEST, preferred_element_type=F32)


def side(*parts):
    return jnp.concatenate(parts, axis=1)


def stack(*parts):
    return jnp.concatenate(parts, axis=0)


def either(flag, if_zero, if_one):
    return jnp.where(flag == 0, if_zero, if_one)


def gram_kernel(basis_ref, high_ref, low_ref, send_ref, keep_ref):
    _, core, _, _ = bits()
    for level in range(LEVELS):
        top = (LEVELS - 1 - level) * RANK
        high, low = split(basis_ref[level * RANK : (level + 1) * RANK, :])
        high_ref[top : top + RANK, :] = high
        low_ref[top : top + RANK, :] = low

    def rows(top, bottom):
        return high_ref[top:bottom, :], low_ref[top:bottom, :]

    a = mm3(rows(320, 576), rows(0, 512), NT)
    b = mm3(rows(64, 320), rows(0, 256), NT)
    row3, row4, row5, row6, row7 = a[:64], b[192:], b[128:192], b[64:128], b[:64]
    slabs_a = side(row3[:, :256], side(row3[:, 256:320], row7[:, :64]), row4[:, :128])
    slabs_b = side(row4[:, 128:], row5[:, :256], row6[:, :128])
    send_ref[:192, :] = a[64:]
    keep_ref[:192, :] = a[64:]
    send_ref[192:, :] = either(core, slabs_b, slabs_a)
    keep_ref[192:, :] = either(core, slabs_a, slabs_b)


def gram_core_kernel(keep_ref, got_ref, low_ref, slab_send_ref, slab_keep_ref):
    _, _, part, _ = bits()
    low_ref[:, :384] = keep_ref[:64, :384] + got_ref[:64, :384]
    low_ref[:, 384:832] = keep_ref[64:128, :448] + got_ref[64:128, :448]
    slabs = keep_ref[192:, :] + got_ref[192:, :]
    slab_send_ref[...] = either(part, slabs[:, 256:], slabs[:, :256])
    slab_keep_ref[...] = either(part, slabs[:, :256], slabs[:, 256:])


def slab_y_kernel(keep_ref, got_ref, send_ref, next_ref):
    _, _, _, y_high = bits()
    slabs = keep_ref[...] + got_ref[...]
    send_ref[...] = either(y_high, slabs[:, 128:], slabs[:, :128])
    next_ref[...] = either(y_high, slabs[:, :128], slabs[:, 128:])


def add_kernel(a_ref, b_ref, out_ref):
    out_ref[...] = a_ref[...] + b_ref[...]


def slab_z_kernel(level, fresh, *refs):
    if fresh:
        slab_ref, got_ref, next_ref, kept_ref = refs
    else:
        slab_ref, got_ref, old_ref, next_ref, kept_ref = refs
    _, core, part, y_high = bits()
    place = core * 4 + part * 2 + y_high
    own, other = slab_ref[...], got_ref[...]
    lane = lax.broadcasted_iota(jnp.int32, own.shape, 1)

    def levels_of(table):
        value = jnp.int32(table[0])
        for index in range(1, 8):
            value = jnp.where(place == index, table[index], value)
        return value

    at = jnp.where(lane < RANK, levels_of(SLAB_FIRST), levels_of(SLAB_SECOND))
    here = at == level
    total = own + other
    old_own = jnp.zeros_like(own) if fresh else old_ref[:, :128]
    old_other = jnp.zeros_like(own) if fresh else old_ref[:, 128:]
    if level == 6:
        old_own = jnp.where(at == 7, total, old_own)
    kept_ref[:, :128] = jnp.where(here, own, old_own)
    kept_ref[:, 128:] = jnp.where(here, other, old_other)
    next_ref[...] = total


def merge_kernel(which, mine_ref, got_ref, out_ref):
    flag = bits()[which]
    mine, got = mine_ref[...], got_ref[...]
    out_ref[...] = either(flag, stack(mine, got), stack(got, mine))


def gather_octet(array):
    for which, mask in ((3, 6), (2, 2), (1, 1)):
        got = sent(array, mask)
        rows, lanes = array.shape
        array, = call(functools.partial(merge_kernel, which), [(2 * rows, lanes)], array, got)
    return array


def solve_kernel(theirs, rhs_ref, inverse_ref, high_ref, low_ref, iterate_ref, terms_ref):
    _, core, _, _ = bits()
    half = 1 - core if theirs else core
    columns = rhs_ref[:, pl.ds(pl.multiple_of(half * 256, 256), 256)]
    iterate = mm3(split(inverse_ref[...]), split(columns), NN)
    iterate_ref[...] = iterate
    terms_ref[...] = mm3(split(iterate.T), (high_ref[...], low_ref[...]), NT)


def caps_kernel(caps_ref, out_ref):
    d, _, _, _ = bits()
    for level in range(LEVELS):
        cap = caps_ref[level]
        turned = stack(cap[RANK:], cap[:RANK])
        turned = side(turned[:, RANK:], turned[:, :RANK])
        out_ref[level] = either(d >> level & 1, cap, turned)


def basis_kernel(basis_ref, high_ref, low_ref):
    high_ref[...], low_ref[...] = split(basis_ref[...].T)


def solved(own, other, cap):
    keep = own.shape[1] - RANK
    return small(side(own[:, keep:], other[:, keep:]), cap, NT)


def rest_of(own, other, both, gram_own, gram_other):
    keep = own.shape[1] - RANK
    return own[:, :keep] + other[:, :keep] - small(both, stack(gram_own, gram_other), NN)


def level0_kernel(own_ref, got_ref, keep_ref, gram_ref, caps_ref, both_ref, send_ref, next_ref):
    _, _, part, _ = bits()
    own, other = own_ref[...], got_ref[...]
    both = solved(own, other, caps_ref[0])
    both_ref[...] = both
    rest = rest_of(own, other, both, keep_ref[128:192, :], gram_ref[128:192, :])
    send_ref[...] = either(part, rest[128:], rest[:128])
    next_ref[...] = either(part, rest[:128], rest[128:])


def level1_kernel(own_ref, got_ref, low_ref, low_got_ref, caps_ref, both_ref, send_ref, next_ref):
    _, _, _, y_high = bits()
    own, other = own_ref[...], got_ref[...]
    both = solved(own, other, caps_ref[1])
    both_ref[...] = both
    rest = rest_of(own, other, both, low_ref[:, 384:832], low_got_ref[:, 384:832])
    gram2 = low_ref[:, :384] + low_got_ref[:, :384]
    send_ref[:, :384] = gram2
    send_ref[:, 384:832] = either(y_high, rest[64:], rest[:64])
    next_ref[:, :384] = gram2
    next_ref[:, 384:832] = either(y_high, rest[:64], rest[64:])


def level2_kernel(own_ref, got_ref, caps_ref, both_ref, next_ref):
    own, other = own_ref[:, 384:832], got_ref[:, 384:832]
    both = solved(own, other, caps_ref[2])
    both_ref[...] = both
    next_ref[...] = rest_of(own, other, both, own_ref[:, :384], got_ref[:, :384])


def gram_rows(gathered, level, shift):
    lanes = slice(shift, shift + 128)
    if level == 3:
        return side(gathered[0:64, lanes], gathered[64:128, lanes],
                    gathered[128:192, shift : shift + 64])
    if level == 4:
        return side(gathered[192:256, lanes], gathered[256:320, lanes])
    if level == 5:
        return side(gathered[320:384, lanes], gathered[384:448, shift : shift + 64])
    return gathered[448:512, lanes]


def middle_kernel(level, own_ref, got_ref, gram_ref, caps_ref, both_ref, next_ref):
    own, other = own_ref[...], got_ref[...]
    both = solved(own, other, caps_ref[level])
    both_ref[...] = both
    rest = rest_of(own, other, both, gram_rows(gram_ref, level, 0), gram_rows(gram_ref, level, 128))
    if level < 6:
        next_ref[...] = rest
    else:
        next_ref[:, :128] = rest
        next_ref[:, 128:] = gram_ref[128:192, :128]


def level7_kernel(own_ref, got_ref, caps_ref, both_ref, next_ref):
    own, other = own_ref[:, :128], got_ref[:, :128]
    both = solved(own, other, caps_ref[7])
    both_ref[...] = both
    next_ref[...] = rest_of(own, other, both, own_ref[:, 192:], got_ref[:, 192:])


def level8_kernel(own_ref, got_ref, both7_ref, caps_ref, out_ref):
    both = solved(own_ref[...], got_ref[...], caps_ref[8])
    out_ref[...] = side(both7_ref[:, :RANK], both[:, :RANK])


def down2_kernel(both2_ref, both3_ref, both4_ref, both5_ref, both6_ref, out_ref):
    out_ref[...] = side(both2_ref[:, RANK:], both3_ref[:, :RANK], both4_ref[:, :RANK],
                        both5_ref[:, :RANK], both6_ref[:, :RANK])


def down1_kernel(mine_ref, got_ref, both2_ref, both1_ref, out_ref):
    _, _, _, y_high = bits()
    own2 = side(both2_ref[:, :RANK], mine_ref[:, RANK:])
    got = got_ref[...]
    rows = either(y_high, stack(own2, got), stack(got, own2))
    out_ref[...] = side(both1_ref[:, RANK:], rows)


def down0_kernel(mine_ref, got_ref, both1_ref, both0_ref, out_ref):
    _, _, part, _ = bits()
    own1 = side(both1_ref[:, :RANK], mine_ref[:, RANK:])
    got = got_ref[...]
    rows = either(part, stack(own1, got), stack(got, own1))
    out_ref[...] = side(both0_ref[:, RANK:], rows)


def first_kernel(mine_ref, got_ref, both0_ref, theirs_ref, own_ref, high_ref, low_ref, out_ref):
    _, core, _, _ = bits()
    own0 = side(both0_ref[:, :RANK], mine_ref[:, RANK:])
    got = got_ref[...]
    factors = (high_ref[:, :448], low_ref[:, :448])
    mine = own_ref[...] - mm3(factors, split(own0), NT)
    other = theirs_ref[...] - mm3(factors, split(got), NT)
    out_ref[:, :256] = either(core, mine, other)
    out_ref[:, 256:] = either(core, other, mine)


def last_kernel(iterate_ref, mine_ref, got_ref, high_ref, low_ref, out_ref):
    _, core, _, _ = bits()
    mine, got = mine_ref[...], got_ref[...]
    rows = either(core, stack(mine, got), stack(got, mine))
    out_ref[...] = iterate_ref[...] - mm3(
        (high_ref[:, 448:], low_ref[:, 448:]), split(rows), NT
    )


def local(rhs, leaf_inverse, basis, caps):
    high, low, gram_send, gram_keep = call(
        gram_kernel, [((576, 512), BF16), ((576, 512), BF16), (256, 512), (256, 512)],
        basis.T, flops=6 * 100_000_000,
    )
    gram_got = sent(gram_send, PARTNER[0])
    iterate_theirs, terms_theirs = call(
        functools.partial(solve_kernel, True), [(512, 256), (256, 576)],
        rhs, leaf_inverse, high, low, flops=6 * 142_000_000,
    )
    terms_got = sent(terms_theirs, PARTNER[0])
    low_sum, slab_send, slab = call(
        gram_core_kernel, [(64, 832), (64, 256), (64, 256)], gram_keep, gram_got
    )
    slab_got = sent(slab_send, PARTNER[1])
    low_got = sent(low_sum, PARTNER[1])
    iterate_own, terms = call(
        functools.partial(solve_kernel, False), [(512, 256), (256, 576)],
        rhs, leaf_inverse, high, low, flops=6 * 142_000_000,
    )
    caps, = call(caps_kernel, [(9, 128, 128)], caps[0])
    both0, send1, state = call(
        level0_kernel, [(256, 128), (128, 512), (128, 512)],
        terms, terms_got, gram_keep, gram_got, caps,
    )
    got1 = sent(send1, PARTNER[1])
    slab_send, slab = call(slab_y_kernel, [(64, 128), (64, 128)], slab, slab_got)
    slab_got = sent(slab_send, PARTNER[2])
    slab, = call(add_kernel, [(64, 128)], slab, slab_got)
    slab_got = sent(slab, PARTNER[3])
    slab, kept = call(
        functools.partial(slab_z_kernel, 3, True), [(64, 128), (64, 256)], slab, slab_got
    )
    slab_got = sent(slab, PARTNER[4])
    slab, kept = call(
        functools.partial(slab_z_kernel, 4, False), [(64, 128), (64, 256)], slab, slab_got, kept
    )
    grams34 = gather_octet(kept)
    slab_got = sent(slab, PARTNER[5])
    slab, kept = call(
        functools.partial(slab_z_kernel, 5, True), [(64, 128), (64, 256)], slab, slab_got
    )
    slab_got = sent(slab, PARTNER[6])
    slab, kept = call(
        functools.partial(slab_z_kernel, 6, False), [(64, 128), (64, 256)], slab, slab_got, kept
    )
    grams567 = gather_octet(kept)

    both1, send2, keep2 = call(
        level1_kernel, [(128, 128), (64, 832), (64, 832)], state, got1, low_sum, low_got, caps
    )
    got2 = sent(send2, PARTNER[2])
    both2, state = call(level2_kernel, [(64, 128), (64, 384)], keep2, got2, caps)
    boths = []
    for level in range(3, 7):
        got = sent(state, PARTNER[level])
        keep = (LEVELS - 1 - level) * RANK if level < 6 else 256
        both, state = call(
            functools.partial(middle_kernel, level), [(64, 128), (64, keep)],
            state, got, grams34 if level < 5 else grams567, caps,
        )
        boths.append(both)
    got = sent(state, PARTNER[7])
    both7, state = call(level7_kernel, [(64, 128), (64, 64)], state, got, caps)
    got = sent(state, PARTNER[8])
    last, = call(level8_kernel, [(64, 128)], state, got, both7, caps)

    basis_high, basis_low = call(basis_kernel, [((512, 576), BF16), ((512, 576), BF16)], basis.T)
    down, = call(down2_kernel, [(64, 320)], both2, *boths)
    got = sent(down, PARTNER[2])
    down, = call(down1_kernel, [(128, 384)], down, got, both2, both1)
    got = sent(down, PARTNER[1])
    down, = call(down0_kernel, [(256, 448)], down, got, both1, both0)
    got = sent(down, PARTNER[0])
    iterate, = call(
        first_kernel, [(512, 512)], down, got, both0, iterate_theirs, iterate_own,
        basis_high, basis_low, flops=6 * 117_000_000,
    )

    for which, mask in ((3, 6), (2, 2)):
        got = sent(last, mask)
        last, = call(
            functools.partial(merge_kernel, which), [(2 * last.shape[0], 128)], last, got
        )
    got = sent(last, PARTNER[0])
    out, = call(
        last_kernel, [(512, 512)], iterate, last, got, basis_high, basis_low, flops=6 * 34_000_000
    )
    return out


def solution(mesh):
    return jax.shard_map(
        local,
        mesh=mesh,
        in_specs=(P("leaf", None), P("leaf", None), P("leaf", None), P("leaf", None, None, None)),
        out_specs=P("leaf", None),
        check_vma=False,
    )
```

```python
import functools

import jax
import jax.numpy as jnp
from jax import lax
from jax.experimental import pallas as pl
from jax.experimental.pallas import tpu as pltpu
from jax.sharding import PartitionSpec as P

HIGHEST = lax.Precision.HIGHEST
F32 = jnp.float32
BF16 = jnp.bfloat16
RANK = 64
LEVELS = 9
PARTNER = (1, 2, 6, 8, 16, 32, 96, 128, 384)
NN, NT = ((1,), (0,)), ((1,), (1,))


def bits():
    d = lax.axis_index("leaf")
    core, y_low, y_high = d & 1, d >> 1 & 1, d >> 2 & 1
    return d, core, y_low ^ y_high, y_high


def sent(array, mask):
    count = lax.axis_size("leaf")
    return lax.ppermute(array, "leaf", [(i, i ^ mask) for i in range(count)])


def call(body, outs, *args, tokens=(), flops=0, grant=6):
    vmem = pl.BlockSpec(memory_space=pltpu.VMEM)
    shapes = [jax.ShapeDtypeStruct(o[0], o[1]) if isinstance(o[0], tuple) else
              jax.ShapeDtypeStruct(o, F32) for o in outs]
    count, after = len(args), len(args) + len(tokens)

    def kernel(*refs):
        body(*refs[:count], *refs[after:])

    moved = sum(a.size * a.dtype.itemsize for a in args)
    return pl.pallas_call(
        kernel,
        out_shape=shapes,
        in_specs=[vmem] * after,
        out_specs=[vmem] * len(outs),
        compiler_params=pltpu.CompilerParams(vmem_limit_bytes=grant * 2**20),
        cost_estimate=pl.CostEstimate(flops=flops, bytes_accessed=moved, transcendentals=0),
    )(*args, *tokens)


def mm(a, b, dims):
    return lax.dot_general(a, b, (dims, ((), ())), preferred_element_type=F32)


def split(x):
    high = x.astype(BF16)
    return high, (x - high.astype(F32)).astype(BF16)


def mm3(a, b, dims):
    return mm(a[0], b[0], dims) + (mm(a[0], b[1], dims) + mm(a[1], b[0], dims))


def small(a, b, dims):
    return lax.dot_general(a, b, (dims, ((), ())), precision=HIGHEST, preferred_element_type=F32)


def side(*parts):
    return jnp.concatenate(parts, axis=1)


def stack(*parts):
    return jnp.concatenate(parts, axis=0)


def either(flag, if_zero, if_one):
    return jnp.where(flag == 0, if_zero, if_one)


def gram_kernel(basis_ref, high_ref, low_ref, send_ref, keep_ref):
    _, core, _, _ = bits()
    for level in range(LEVELS):
        top = (LEVELS - 1 - level) * RANK
        high, low = split(basis_ref[level * RANK : (level + 1) * RANK, :])
        high_ref[top : top + RANK, :] = high
        low_ref[top : top + RANK, :] = low

    def rows(top, bottom):
        return high_ref[top:bottom, :], low_ref[top:bottom, :]

    a = mm3(rows(320, 576), rows(0, 512), NT)
    b = mm3(rows(64, 320), rows(0, 256), NT)
    row3, row4, row5, row6, row7 = a[:64], b[192:], b[128:192], b[64:128], b[:64]
    first = side(row3[:, :128], side(row3[:, 256:320], row7[:, :64]), row4[:, :128], row5[:, :128])
    second = side(row3[:, 128:256], row4[:, 128:], row5[:, 128:256], row6[:, :128])
    send_ref[:192, :] = a[64:]
    keep_ref[:192, :] = a[64:]
    send_ref[192:, :] = either(core, second, first)
    keep_ref[192:, :] = either(core, first, second)


def gram_core_kernel(keep_ref, got_ref, out_ref):
    out_ref[:, :512] = keep_ref[192:, :] + got_ref[192:, :]
    out_ref[:, 512:896] = keep_ref[:64, :384] + got_ref[:64, :384]
    out_ref[:, 896:] = keep_ref[64:128, :] + got_ref[64:128, :]


def gram_add_kernel(own_ref, got_ref, out_ref):
    lanes = out_ref.shape[1]
    out_ref[...] = own_ref[:, :lanes] + got_ref[:, :lanes]


def gram_level_kernel(level, own_ref, got_ref, swap_ref, next_ref=None):
    _, core, _, _ = bits()
    own, other = own_ref[...], got_ref[...]
    total = own + other
    if level == 3:
        swap_ref[:, :256] = side(own[:, :128], other[:, :128])
        swap_ref[:, 256:] = side(own[:, 128:192], other[:, 128:192])
        next_ref[...] = total[:, 128:]
    elif level == 4:
        swap_ref[:, :128] = either(core, own[:, 128:256], own[:, :128])
        swap_ref[:, 128:] = either(core, other[:, 128:256], other[:, :128])
        next_ref[:, :128] = either(core, total[:, :128], total[:, 128:256])
        next_ref[:, 128:] = total[:, 256:]
    elif level == 5:
        swap_ref[:, :128] = either(core, own[:, 128:], own[:, :128])
        swap_ref[:, 128:] = either(core, other[:, 128:], other[:, :128])
        next_ref[...] = either(core, total[:, :128], total[:, 128:])
    else:
        swap_ref[:, :128] = either(core, total, own)
        swap_ref[:, 128:] = other


GRAM_OUTS = {
    3: [(64, 384), (64, 384)],
    4: [(64, 256), (64, 256)],
    5: [(64, 256), (64, 128)],
    6: [(64, 256)],
}


def gram_rows(level, first, second):
    if level == 3:
        return (side(first[:, :128], second[:, :128], first[:, 256:320]),
                side(first[:, 128:256], second[:, 128:256], first[:, 320:384]))
    if level == 4:
        return side(first[:, :128], second[:, :128]), side(first[:, 128:], second[:, 128:])
    if level == 5:
        return side(first[:, :128], second[:, :64]), side(first[:, 128:], second[:, 128:192])
    return second[:, :128], second[:, 128:]


def solve_kernel(theirs, rhs_ref, inverse_ref, high_ref, low_ref, iterate_ref, terms_ref):
    _, core, _, _ = bits()
    half = 1 - core if theirs else core
    columns = rhs_ref[:, pl.ds(pl.multiple_of(half * 256, 256), 256)]
    iterate = mm3(split(inverse_ref[...]), split(columns), NN)
    iterate_ref[...] = iterate
    terms_ref[:, :576] = mm3(split(iterate.T), (high_ref[...], low_ref[...]), NT)
    terms_ref[:, 576:] = jnp.zeros((256, 64), F32)


def caps_kernel(caps_ref, out_ref):
    d, _, _, _ = bits()
    for level in range(LEVELS):
        cap = caps_ref[level]
        turned = stack(cap[RANK:], cap[:RANK])
        turned = side(turned[:, RANK:], turned[:, :RANK])
        out_ref[level] = either(d >> level & 1, cap, turned)


def basis_kernel(basis_ref, high_ref, low_ref):
    high_ref[...], low_ref[...] = split(basis_ref[...].T)


def solved(own, other, cap):
    keep = own.shape[1] - RANK
    return small(side(own[:, keep:], other[:, keep:]), cap, NT)


def rest_of(own, other, both, gram_own, gram_other):
    keep = own.shape[1] - RANK
    return own[:, :keep] + other[:, :keep] - small(both, stack(gram_own, gram_other), NN)


def level0_kernel(own_ref, got_ref, keep_ref, gram_ref, caps_ref, both_ref, send_ref, next_ref):
    _, _, part, _ = bits()
    own, other = own_ref[:, :576], got_ref[:, :576]
    both = solved(own, other, caps_ref[0])
    both_ref[...] = both
    rest = rest_of(own, other, both, keep_ref[128:192, :], gram_ref[128:192, :])
    send_ref[...] = either(part, rest[128:], rest[:128])
    next_ref[...] = either(part, rest[:128], rest[128:])


def level1_kernel(own_ref, got_ref, low_ref, low_got_ref, caps_ref, both_ref, send_ref, next_ref):
    _, _, _, y_high = bits()
    own, other = own_ref[...], got_ref[...]
    both = solved(own, other, caps_ref[1])
    both_ref[...] = both
    rest = rest_of(own, other, both, low_ref[:, 896:1344], low_got_ref[:, 896:1344])
    send_ref[:, :448] = either(y_high, rest[64:], rest[:64])
    next_ref[:, :448] = either(y_high, rest[:64], rest[64:])
    send_ref[:, 448:] = jnp.zeros((64, 64), F32)
    next_ref[:, 448:] = jnp.zeros((64, 64), F32)


def level2_kernel(own_ref, got_ref, low_ref, low_got_ref, caps_ref, both_ref, next_ref):
    own, other = own_ref[:, :448], got_ref[:, :448]
    both = solved(own, other, caps_ref[2])
    both_ref[...] = both
    next_ref[...] = rest_of(own, other, both, low_ref[:, 512:896], low_got_ref[:, 512:896])


def middle_kernel(level, own_ref, got_ref, swap_ref, swap_got_ref, caps_ref, both_ref, next_ref):
    width = (LEVELS - level) * RANK
    own, other = own_ref[:, :width], got_ref[:, :width]
    both = solved(own, other, caps_ref[level])
    both_ref[...] = both
    _, core, _, _ = bits()
    mine, got = swap_ref[...], swap_got_ref[...]
    first, second = either(core, mine, got), either(core, got, mine)
    rest = rest_of(own, other, both, *gram_rows(level, first, second))
    if level < 6:
        next_ref[:, : width - RANK] = rest
        if next_ref.shape[1] > width - RANK:
            next_ref[:, width - RANK :] = jnp.zeros((64, RANK), F32)
    else:
        next_ref[:, :128] = rest
        next_ref[:, 128:] = first[:, :128]


def level7_kernel(own_ref, got_ref, caps_ref, both_ref, next_ref):
    own, other = own_ref[:, :128], got_ref[:, :128]
    both = solved(own, other, caps_ref[7])
    both_ref[...] = both
    rest = rest_of(own, other, both, own_ref[:, 192:], got_ref[:, 192:])
    next_ref[...] = side(rest, jnp.zeros((64, RANK), F32))


def level8_kernel(own_ref, got_ref, both5_ref, both6_ref, both7_ref, caps_ref, out_ref):
    both = solved(own_ref[:, :RANK], got_ref[:, :RANK], caps_ref[8])
    out_ref[:, :128] = side(both5_ref[:, :RANK], both6_ref[:, :RANK])
    out_ref[:, 128:] = side(both7_ref[:, :RANK], both[:, :RANK])


def down2_kernel(both2_ref, both3_ref, both4_ref, out_ref):
    out_ref[:, :128] = side(both2_ref[:, RANK:], both3_ref[:, :RANK])
    out_ref[:, 128:] = both4_ref[...]


def down1_kernel(mine_ref, got_ref, both2_ref, both1_ref, out_ref):
    _, _, _, y_high = bits()
    own = side(both2_ref[:, :RANK], mine_ref[:, RANK:192])
    got = got_ref[:, :192]
    out_ref[...] = side(both1_ref[:, RANK:], either(y_high, stack(own, got), stack(got, own)))


def down0_kernel(mine_ref, got_ref, both1_ref, out_ref):
    _, _, part, _ = bits()
    own = side(both1_ref[:, :RANK], mine_ref[:, RANK:])
    got = got_ref[...]
    out_ref[...] = either(part, stack(own, got), stack(got, own))


def tail_kernel(mine_ref, far_high_ref, far_low_ref, across_ref, down_ref, both0_ref,
                send_ref, own_ref):
    _, _, part, y_high = bits()
    mine, far_high = mine_ref[...], far_high_ref[...]
    far_low, across = far_low_ref[...], across_ref[...]
    near = either(y_high, stack(mine, far_high), stack(far_high, mine))
    other = either(y_high, stack(far_low, across), stack(across, far_low))
    last = either(part, stack(near, other), stack(other, near))
    rest = side(down_ref[...], last)
    send_ref[:, :576] = side(both0_ref[:, RANK:], rest)
    send_ref[:, 576:] = jnp.zeros((256, 64), F32)
    own_ref[:, :576] = side(both0_ref[:, :RANK], rest)
    own_ref[:, 576:] = jnp.zeros((256, 64), F32)


def final_half_kernel(iterate_ref, corrections_ref, high_ref, low_ref, out_ref):
    out_ref[...] = iterate_ref[...] - mm3(
        (high_ref[...], low_ref[...]), split(corrections_ref[:, :576]), NT
    )


def final_kernel(iterate_ref, corrections_ref, high_ref, low_ref, half_ref, out_ref):
    _, core, _, _ = bits()
    other = iterate_ref[...] - mm3(
        (high_ref[...], low_ref[...]), split(corrections_ref[:, :576]), NT
    )
    half = half_ref[...]
    out_ref[:, :256] = either(core, half, other)
    out_ref[:, 256:] = either(core, other, half)


def local(rhs, leaf_inverse, basis, caps):
    partial = functools.partial
    high, low, gram_send, gram_keep = call(
        gram_kernel, [((576, 512), BF16), ((576, 512), BF16), (256, 512), (256, 512)],
        basis.T, flops=6 * 100_000_000, grant=12,
    )
    gram_got = sent(gram_send, PARTNER[0])
    iterate_theirs, terms_theirs = call(
        partial(solve_kernel, True), [(512, 256), (256, 640)],
        rhs, leaf_inverse, high, low, flops=6 * 142_000_000, grant=12,
    )
    terms_got = sent(terms_theirs, PARTNER[0])
    gram1, = call(gram_core_kernel, [(64, 1408)], gram_keep, gram_got, tokens=(terms_theirs,))
    gram1_got = sent(gram1, PARTNER[1])
    iterate_own, terms = call(
        partial(solve_kernel, False), [(512, 256), (256, 640)],
        rhs, leaf_inverse, high, low, tokens=(gram1,), flops=6 * 142_000_000, grant=12,
    )
    caps, = call(caps_kernel, [(9, 128, 128)], caps[0])
    both0, send1, state = call(
        level0_kernel, [(256, 128), (128, 512), (128, 512)],
        terms, terms_got, gram_keep, gram_got, caps,
    )
    got = sent(send1, PARTNER[1])
    gram2, = call(gram_add_kernel, [(64, 896)], gram1, gram1_got, tokens=(send1,))
    gram2_got = sent(gram2, PARTNER[2])
    both1, send2, state = call(
        level1_kernel, [(128, 128), (64, 512), (64, 512)], state, got, gram1, gram1_got, caps
    )
    got = sent(send2, PARTNER[2])
    gram, = call(gram_add_kernel, [(64, 512)], gram2, gram2_got, tokens=(send2,))
    grams = gram, sent(gram, PARTNER[3])
    both2, state = call(
        level2_kernel, [(64, 128), (64, 384)], state, got, gram2, gram2_got, caps
    )
    basis_high, basis_low = call(
        basis_kernel, [((512, 576), BF16), ((512, 576), BF16)], basis.T, tokens=(state,)
    )
    boths = []
    for level in range(3, 7):
        got = sent(state, PARTNER[level])
        swap, *gram = call(
            partial(gram_level_kernel, level), GRAM_OUTS[level], *grams, tokens=(state,)
        )
        swap_got = sent(swap, PARTNER[0])
        if level < 6:
            grams = gram[0], sent(gram[0], PARTNER[level + 1])
        if level == 5:
            down, = call(down2_kernel, [(64, 256)], both2, *boths)
            down_got = sent(down, PARTNER[2])
        if level == 6:
            down, = call(
                down1_kernel, [(128, 256)], down, down_got, both2, both1, tokens=(state,)
            )
            down_got = sent(down, PARTNER[1])
        both, state = call(
            partial(middle_kernel, level), [(64, 128), (64, {3: 384, 4: 256, 5: 256, 6: 256}[level])],
            state, got, swap, swap_got, caps, tokens=(basis_low,) if level == 4 else (),
        )
        boths.append(both)
    got = sent(state, PARTNER[7])
    both7, state = call(level7_kernel, [(64, 128), (64, 128)], state, got, caps)
    got = sent(state, PARTNER[8])
    down, = call(down0_kernel, [(256, 256)], down, down_got, both1, tokens=(state,))
    last, = call(level8_kernel, [(64, 256)], state, got, *boths[2:], both7, caps)
    send, own = call(
        tail_kernel, [(256, 640), (256, 640)],
        last, sent(last, 6), sent(last, 2), sent(last, 4), down, both0,
    )
    got = sent(send, PARTNER[0])
    half, = call(
        final_half_kernel, [(512, 256)], iterate_own, own, basis_high, basis_low,
        flops=6 * 75_000_000, grant=12,
    )
    out, = call(
        final_kernel, [(512, 512)], iterate_theirs, got, basis_high, basis_low, half,
        flops=6 * 75_000_000, grant=12,
    )
    return out


def solution(mesh):
    return jax.shard_map(
        local,
        mesh=mesh,
        in_specs=(P("leaf", None), P("leaf", None), P("leaf", None), P("leaf", None, None, None)),
        out_specs=P("leaf", None),
        check_vma=False,
    )
```

```python
import functools

import jax
import jax.numpy as jnp
from jax import lax
from jax.experimental import pallas as pl
from jax.experimental.pallas import tpu as pltpu
from jax.sharding import PartitionSpec as P

HIGHEST = lax.Precision.HIGHEST
F32 = jnp.float32
BF16 = jnp.bfloat16
RANK = 64
LEVELS = 9
PARTNER = (1, 2, 6, 8, 16, 32, 96, 128, 384)
NN, NT = ((1,), (0,)), ((1,), (1,))


def bits():
    d = lax.axis_index("leaf")
    core, y_low, y_high = d & 1, d >> 1 & 1, d >> 2 & 1
    return d, core, y_low ^ y_high, y_high


def sent(array, mask):
    count = lax.axis_size("leaf")
    return lax.ppermute(array, "leaf", [(i, i ^ mask) for i in range(count)])


def call(body, outs, *args, tokens=(), flops=0, grant=6):
    vmem = pl.BlockSpec(memory_space=pltpu.VMEM)
    shapes = [jax.ShapeDtypeStruct(o[0], o[1]) if isinstance(o[0], tuple) else
              jax.ShapeDtypeStruct(o, F32) for o in outs]
    count, after = len(args), len(args) + len(tokens)

    def kernel(*refs):
        body(*refs[:count], *refs[after:])

    moved = sum(a.size * a.dtype.itemsize for a in args)
    return pl.pallas_call(
        kernel,
        out_shape=shapes,
        in_specs=[vmem] * after,
        out_specs=[vmem] * len(outs),
        compiler_params=pltpu.CompilerParams(vmem_limit_bytes=grant * 2**20),
        cost_estimate=pl.CostEstimate(flops=flops, bytes_accessed=moved, transcendentals=0),
    )(*args, *tokens)


def mm(a, b, dims):
    return lax.dot_general(a, b, (dims, ((), ())), preferred_element_type=F32)


def split(x):
    high = x.astype(BF16)
    return high, (x - high.astype(F32)).astype(BF16)


def mm3(a, b, dims):
    return mm(a[0], b[0], dims) + (mm(a[0], b[1], dims) + mm(a[1], b[0], dims))


def small(a, b, dims):
    return lax.dot_general(a, b, (dims, ((), ())), precision=HIGHEST, preferred_element_type=F32)


def side(*parts):
    return jnp.concatenate(parts, axis=1)


def stack(*parts):
    return jnp.concatenate(parts, axis=0)


def either(flag, if_zero, if_one):
    return jnp.where(flag == 0, if_zero, if_one)


def gram_kernel(basis_ref, high_ref, low_ref, send_ref, keep_ref):
    _, core, _, _ = bits()
    for level in range(LEVELS):
        top = (LEVELS - 1 - level) * RANK
        high, low = split(basis_ref[level * RANK : (level + 1) * RANK, :])
        high_ref[top : top + RANK, :] = high
        low_ref[top : top + RANK, :] = low

    def rows(top, bottom):
        return high_ref[top:bottom, :], low_ref[top:bottom, :]

    a = mm3(rows(320, 576), rows(0, 512), NT)
    b = mm3(rows(64, 320), rows(0, 256), NT)
    row3, row4, row5, row6, row7 = a[:64], b[192:], b[128:192], b[64:128], b[:64]
    first = side(row3[:, :128], side(row3[:, 256:320], row7[:, :64]), row4[:, :128], row5[:, :128])
    second = side(row3[:, 128:256], row4[:, 128:], row5[:, 128:256], row6[:, :128])
    send_ref[:192, :] = a[64:]
    keep_ref[:192, :] = a[64:]
    send_ref[192:, :] = either(core, second, first)
    keep_ref[192:, :] = either(core, first, second)


def gram_core_kernel(keep_ref, got_ref, out_ref):
    out_ref[:, :512] = keep_ref[192:, :] + got_ref[192:, :]
    out_ref[:, 512:896] = keep_ref[:64, :384] + got_ref[:64, :384]
    out_ref[:, 896:] = keep_ref[64:128, :] + got_ref[64:128, :]


def gram_add_kernel(own_ref, got_ref, out_ref):
    lanes = out_ref.shape[1]
    out_ref[...] = own_ref[:, :lanes] + got_ref[:, :lanes]


def gram_level_kernel(level, own_ref, got_ref, swap_ref, next_ref=None):
    _, core, _, _ = bits()
    own, other = own_ref[...], got_ref[...]
    total = own + other
    if level == 3:
        swap_ref[:, :256] = side(own[:, :128], other[:, :128])
        swap_ref[:, 256:] = side(own[:, 128:192], other[:, 128:192])
        next_ref[...] = total[:, 128:]
    elif level == 4:
        swap_ref[:, :128] = either(core, own[:, 128:256], own[:, :128])
        swap_ref[:, 128:] = either(core, other[:, 128:256], other[:, :128])
        next_ref[:, :128] = either(core, total[:, :128], total[:, 128:256])
        next_ref[:, 128:] = total[:, 256:]
    elif level == 5:
        swap_ref[:, :128] = either(core, own[:, 128:], own[:, :128])
        swap_ref[:, 128:] = either(core, other[:, 128:], other[:, :128])
        next_ref[...] = either(core, total[:, :128], total[:, 128:])
    else:
        swap_ref[:, :128] = either(core, total, own)
        swap_ref[:, 128:] = other


GRAM_OUTS = {
    3: [(64, 384), (64, 384)],
    4: [(64, 256), (64, 256)],
    5: [(64, 256), (64, 128)],
    6: [(64, 256)],
}


def gram_rows(level, first, second):
    if level == 3:
        return (side(first[:, :128], second[:, :128], first[:, 256:320]),
                side(first[:, 128:256], second[:, 128:256], first[:, 320:384]))
    if level == 4:
        return side(first[:, :128], second[:, :128]), side(first[:, 128:], second[:, 128:])
    if level == 5:
        return side(first[:, :128], second[:, :64]), side(first[:, 128:], second[:, 128:192])
    return second[:, :128], second[:, 128:]


def solve_kernel(theirs, rhs_ref, inverse_ref, high_ref, low_ref, iterate_ref, terms_ref):
    _, core, _, _ = bits()
    half = 1 - core if theirs else core
    columns = rhs_ref[:, pl.ds(pl.multiple_of(half * 256, 256), 256)]
    iterate = mm3(split(inverse_ref[...]), split(columns), NN)
    iterate_ref[...] = iterate
    terms_ref[:, :576] = mm3(split(iterate.T), (high_ref[...], low_ref[...]), NT)
    terms_ref[:, 576:] = jnp.zeros((256, 64), F32)


def caps_kernel(caps_ref, out_ref, top_ref):
    d, _, _, _ = bits()
    for level in range(LEVELS):
        cap = caps_ref[level]
        turned = stack(cap[RANK:], cap[:RANK])
        turned = side(turned[:, RANK:], turned[:, :RANK])
        out_ref[level] = either(d >> level & 1, cap, turned)
        if level == 7:
            top_ref[...] = either(d >> level & 1, cap, turned)


def basis_kernel(basis_ref, high_ref, low_ref):
    high_ref[...], low_ref[...] = split(basis_ref[...].T)


def solved(own, other, cap):
    keep = own.shape[1] - RANK
    return small(side(own[:, keep:], other[:, keep:]), cap, NT)


def rest_of(own, other, both, gram_own, gram_other):
    keep = own.shape[1] - RANK
    return own[:, :keep] + other[:, :keep] - small(both, stack(gram_own, gram_other), NN)


def level0_kernel(own_ref, got_ref, keep_ref, gram_ref, caps_ref, both_ref, send_ref, next_ref):
    _, _, part, _ = bits()
    own, other = own_ref[:, :576], got_ref[:, :576]
    both = solved(own, other, caps_ref[0])
    both_ref[...] = both
    rest = rest_of(own, other, both, keep_ref[128:192, :], gram_ref[128:192, :])
    send_ref[...] = either(part, rest[128:], rest[:128])
    next_ref[...] = either(part, rest[:128], rest[128:])


def level1_kernel(own_ref, got_ref, low_ref, low_got_ref, caps_ref, both_ref, send_ref, next_ref):
    _, _, _, y_high = bits()
    own, other = own_ref[...], got_ref[...]
    both = solved(own, other, caps_ref[1])
    both_ref[...] = both
    rest = rest_of(own, other, both, low_ref[:, 896:1344], low_got_ref[:, 896:1344])
    send_ref[:, :448] = either(y_high, rest[64:], rest[:64])
    next_ref[:, :448] = either(y_high, rest[:64], rest[64:])
    send_ref[:, 448:] = jnp.zeros((64, 64), F32)
    next_ref[:, 448:] = jnp.zeros((64, 64), F32)


def level2_kernel(own_ref, got_ref, low_ref, low_got_ref, caps_ref, both_ref, next_ref):
    own, other = own_ref[:, :448], got_ref[:, :448]
    both = solved(own, other, caps_ref[2])
    both_ref[...] = both
    next_ref[...] = rest_of(own, other, both, low_ref[:, 512:896], low_got_ref[:, 512:896])


def middle_kernel(level, own_ref, got_ref, swap_ref, swap_got_ref, caps_ref, both_ref, next_ref):
    width = (LEVELS - level) * RANK
    own, other = own_ref[:, :width], got_ref[:, :width]
    both = solved(own, other, caps_ref[level])
    both_ref[...] = both
    _, core, _, _ = bits()
    mine, got = swap_ref[...], swap_got_ref[...]
    first, second = either(core, mine, got), either(core, got, mine)
    rest = rest_of(own, other, both, *gram_rows(level, first, second))
    if level < 6:
        next_ref[:, : width - RANK] = rest
        if next_ref.shape[1] > width - RANK:
            next_ref[:, width - RANK :] = jnp.zeros((64, RANK), F32)
    else:
        next_ref[:, :128] = rest
        next_ref[:, 128:] = first[:, :128]


def top_kernel(all_ref, cap_ref, caps_ref, both5_ref, both6_ref, out_ref):
    d, _, _, _ = bits()
    x = d >> 7
    blocks = [all_ref[x ^ n] for n in range(4)]
    terms = [block[:, :128] for block in blocks]
    grams = [block[:, 192:] for block in blocks]
    both7 = solved(terms[0], terms[1], caps_ref[7])
    other7 = solved(terms[2], terms[3], cap_ref[...])
    own8 = rest_of(terms[0], terms[1], both7, grams[0], grams[1])
    other8 = rest_of(terms[2], terms[3], other7, grams[2], grams[3])
    both8 = solved(own8, other8, caps_ref[8])
    out_ref[:, :128] = side(both5_ref[:, :RANK], both6_ref[:, :RANK])
    out_ref[:, 128:] = side(both7[:, :RANK], both8[:, :RANK])


def down2_kernel(both2_ref, both3_ref, both4_ref, out_ref):
    out_ref[:, :128] = side(both2_ref[:, RANK:], both3_ref[:, :RANK])
    out_ref[:, 128:] = both4_ref[...]


def down1_kernel(mine_ref, got_ref, both2_ref, both1_ref, out_ref):
    _, _, _, y_high = bits()
    own = side(both2_ref[:, :RANK], mine_ref[:, RANK:192])
    got = got_ref[:, :192]
    out_ref[...] = side(both1_ref[:, RANK:], either(y_high, stack(own, got), stack(got, own)))


def down0_kernel(mine_ref, got_ref, both1_ref, both0_ref, send_ref, own_ref):
    _, _, part, _ = bits()
    own = side(both1_ref[:, :RANK], mine_ref[:, RANK:])
    got = got_ref[...]
    rows = either(part, stack(own, got), stack(got, own))
    send_ref[:, :320] = side(both0_ref[:, RANK:], rows)
    own_ref[:, :320] = side(both0_ref[:, :RANK], rows)
    send_ref[:, 320:] = jnp.zeros((256, 64), F32)
    own_ref[:, 320:] = jnp.zeros((256, 64), F32)


def place(shard):
    core, part, y_high = shard >> 2, shard >> 1 & 1, shard & 1
    return y_high << 2 | (part ^ y_high) << 1 | core


def final_kernel(theirs_ref, mine_ref, got_ref, own_ref, all_ref, high_ref, low_ref, out_ref):
    _, core, _, _ = bits()
    factors = (high_ref[...], low_ref[...])
    last = [all_ref[place(shard)] for shard in range(8)]
    first, second = stack(*last[:4]), stack(*last[4:])
    own = side(own_ref[:, :320], either(core, first, second))
    other = side(got_ref[:, :320], either(core, second, first))
    own_out = mine_ref[...] - mm3(factors, split(own), NT)
    other_out = theirs_ref[...] - mm3(factors, split(other), NT)
    out_ref[:, :256] = either(core, own_out, other_out)
    out_ref[:, 256:] = either(core, other_out, own_out)


def local(rhs, leaf_inverse, basis, caps):
    partial = functools.partial
    high, low, gram_send, gram_keep = call(
        gram_kernel, [((576, 512), BF16), ((576, 512), BF16), (256, 512), (256, 512)],
        basis.T, flops=6 * 100_000_000, grant=12,
    )
    gram_got = sent(gram_send, PARTNER[0])
    iterate_theirs, terms_theirs = call(
        partial(solve_kernel, True), [(512, 256), (256, 640)],
        rhs, leaf_inverse, high, low, flops=6 * 142_000_000, grant=12,
    )
    terms_got = sent(terms_theirs, PARTNER[0])
    gram1, = call(gram_core_kernel, [(64, 1408)], gram_keep, gram_got, tokens=(terms_theirs,))
    gram1_got = sent(gram1, PARTNER[1])
    iterate_own, terms = call(
        partial(solve_kernel, False), [(512, 256), (256, 640)],
        rhs, leaf_inverse, high, low, tokens=(gram1,), flops=6 * 142_000_000, grant=12,
    )
    caps, cap7 = call(caps_kernel, [(9, 128, 128), (128, 128)], caps[0])
    both0, send1, state = call(
        level0_kernel, [(256, 128), (128, 512), (128, 512)],
        terms, terms_got, gram_keep, gram_got, caps,
    )
    got = sent(send1, PARTNER[1])
    cap_got = sent(cap7, 256)
    gram2, = call(gram_add_kernel, [(64, 896)], gram1, gram1_got, tokens=(send1,))
    gram2_got = sent(gram2, PARTNER[2])
    both1, send2, state = call(
        level1_kernel, [(128, 128), (64, 512), (64, 512)], state, got, gram1, gram1_got, caps,
        tokens=(cap_got,),
    )
    got = sent(send2, PARTNER[2])
    gram, = call(gram_add_kernel, [(64, 512)], gram2, gram2_got, tokens=(send2,))
    grams = gram, sent(gram, PARTNER[3])
    both2, state = call(
        level2_kernel, [(64, 128), (64, 384)], state, got, gram2, gram2_got, caps
    )
    basis_high, basis_low = call(
        basis_kernel, [((512, 576), BF16), ((512, 576), BF16)], basis.T, tokens=(state,)
    )
    boths = []
    for level in range(3, 7):
        got = sent(state, PARTNER[level])
        swap, *gram = call(
            partial(gram_level_kernel, level), GRAM_OUTS[level], *grams, tokens=(state,)
        )
        swap_got = sent(swap, PARTNER[0])
        if level < 6:
            grams = gram[0], sent(gram[0], PARTNER[level + 1])
        if level == 5:
            down, = call(down2_kernel, [(64, 256)], both2, *boths)
            down_got = sent(down, PARTNER[2])
        if level == 6:
            down, = call(
                down1_kernel, [(128, 256)], down, down_got, both2, both1, tokens=(state,)
            )
            down_got = sent(down, PARTNER[1])
        both, state = call(
            partial(middle_kernel, level), [(64, 128), (64, {3: 384, 4: 256, 5: 256, 6: 256}[level])],
            state, got, swap, swap_got, caps, tokens=(basis_low,) if level == 4 else (),
        )
        boths.append(both)
    columns = [[n + 128 * x for x in range(4)] for n in range(128)]
    gathered = lax.all_gather(state, "leaf", axis_index_groups=columns)
    down_send, down_own = call(
        down0_kernel, [(256, 384), (256, 384)], down, down_got, both1, both0, tokens=(gathered,)
    )
    down_got = sent(down_send, PARTNER[0])
    last, = call(
        top_kernel, [(64, 256)], gathered, cap_got, caps, *boths[2:], tokens=(down_own,)
    )
    octets = [list(range(n, n + 8)) for n in range(0, 512, 8)]
    gathered = lax.all_gather(last, "leaf", axis_index_groups=octets)
    out, = call(
        final_kernel, [(512, 512)], iterate_theirs, iterate_own, down_got, down_own, gathered,
        basis_high, basis_low, flops=12 * 75_000_000, grant=16,
    )
    return out


def solution(mesh):
    return jax.shard_map(
        local,
        mesh=mesh,
        in_specs=(P("leaf", None), P("leaf", None), P("leaf", None), P("leaf", None, None, None)),
        out_specs=P("leaf", None),
        check_vma=False,
    )
```

```python
import functools

import jax
import jax.numpy as jnp
from jax import lax
from jax.experimental import pallas as pl
from jax.experimental.pallas import tpu as pltpu
from jax.sharding import PartitionSpec as P

HIGHEST = lax.Precision.HIGHEST
F32 = jnp.float32
BF16 = jnp.bfloat16
RANK = 64
LEVELS = 9
PARTNER = (1, 2, 6, 8, 16, 32, 96, 128, 384)
NN, NT = ((1,), (0,)), ((1,), (1,))


def bits():
    d = lax.axis_index("leaf")
    core, y_low, y_high = d & 1, d >> 1 & 1, d >> 2 & 1
    return d, core, y_low ^ y_high, y_high


def sent(array, mask):
    count = lax.axis_size("leaf")
    return lax.ppermute(array, "leaf", [(i, i ^ mask) for i in range(count)])


def call(body, outs, *args, tokens=(), flops=0, grant=6):
    vmem = pl.BlockSpec(memory_space=pltpu.VMEM)
    shapes = [jax.ShapeDtypeStruct(o[0], o[1]) if isinstance(o[0], tuple) else
              jax.ShapeDtypeStruct(o, F32) for o in outs]
    count, after = len(args), len(args) + len(tokens)

    def kernel(*refs):
        body(*refs[:count], *refs[after:])

    moved = sum(a.size * a.dtype.itemsize for a in args)
    return pl.pallas_call(
        kernel,
        out_shape=shapes,
        in_specs=[vmem] * after,
        out_specs=[vmem] * len(outs),
        compiler_params=pltpu.CompilerParams(vmem_limit_bytes=grant * 2**20),
        cost_estimate=pl.CostEstimate(flops=flops, bytes_accessed=moved, transcendentals=0),
    )(*args, *tokens)


def mm(a, b, dims):
    return lax.dot_general(a, b, (dims, ((), ())), preferred_element_type=F32)


def split(x):
    high = x.astype(BF16)
    return high, (x - high.astype(F32)).astype(BF16)


def mm3(a, b, dims):
    return mm(a[0], b[0], dims) + (mm(a[0], b[1], dims) + mm(a[1], b[0], dims))


def small(a, b, dims):
    return lax.dot_general(a, b, (dims, ((), ())), precision=HIGHEST, preferred_element_type=F32)


def side(*parts):
    return jnp.concatenate(parts, axis=1)


def stack(*parts):
    return jnp.concatenate(parts, axis=0)


def either(flag, if_zero, if_one):
    return jnp.where(flag == 0, if_zero, if_one)


def folded(x):
    full = x.shape[1] // 128
    parts = [x[:, 128 * i : 128 * (i + 1)] for i in range(full)]
    last = x[:, 128 * full :]
    return stack(*parts, side(last[:32], last[32:]))


def unfolded(x):
    full = x.shape[0] // 64
    parts = [x[64 * i : 64 * (i + 1)] for i in range(full)]
    last = x[64 * full :]
    return side(*parts, stack(last[:, :64], last[:, 64:]))


def gram_kernel(basis_ref, high_ref, low_ref, send_ref, keep_ref):
    _, core, _, _ = bits()
    for level in range(LEVELS):
        top = (LEVELS - 1 - level) * RANK
        high, low = split(basis_ref[level * RANK : (level + 1) * RANK, :])
        high_ref[top : top + RANK, :] = high
        low_ref[top : top + RANK, :] = low

    def rows(top, bottom):
        return high_ref[top:bottom, :], low_ref[top:bottom, :]

    a = mm3(rows(320, 576), rows(0, 512), NT)
    b = mm3(rows(64, 320), rows(0, 256), NT)
    row3, row4, row5, row6, row7 = a[:64], b[192:], b[128:192], b[64:128], b[:64]
    first = side(
        row4[:, :128], side(row5[:, :64], row6[:, :64]), side(row7[:, :64], row3[:, 256:320]),
        row3[:, :128],
    )
    second = side(
        row4[:, 128:], side(row5[:, 64:128], row6[:, 64:128]), row5[:, 128:256], row3[:, 128:256]
    )
    send_ref[:192, :] = a[64:]
    keep_ref[:192, :] = a[64:]
    send_ref[192:, :] = either(core, second, first)
    keep_ref[192:, :] = either(core, first, second)


def gram_core_kernel(keep_ref, got_ref, out_ref):
    out_ref[:, :512] = keep_ref[192:, :] + got_ref[192:, :]
    out_ref[:, 512:896] = keep_ref[:64, :384] + got_ref[:64, :384]
    out_ref[:, 896:] = keep_ref[64:128, :] + got_ref[64:128, :]


def gram_add_kernel(own_ref, got_ref, out_ref):
    lanes = out_ref.shape[1]
    out_ref[...] = own_ref[:, :lanes] + got_ref[:, :lanes]


def gram_level_kernel(level, own_ref, got_ref, swap_ref, next_ref=None, send_ref=None):
    _, core, _, _ = bits()
    own, other = own_ref[...], got_ref[...]
    if level in (4, 5):
        other = unfolded(other)
    total = own + other
    if level == 3:
        swap_ref[:, :256] = side(own[:, 384:], other[:, 384:])
        swap_ref[:, 256:] = side(own[:, 320:384], other[:, 320:384])
        rest = total[:, :320]
    elif level == 4:
        swap_ref[...] = side(own[:, :128], other[:, :128])
        rest = total[:, 128:]
    elif level == 5:
        swap_ref[:, :128] = either(core, own[:, :128], side(own[:, :64], own[:, 128:]))
        swap_ref[:, 128:] = either(core, other[:, :128], side(other[:, :64], other[:, 128:]))
        next_ref[...] = total[:, 64:]
    else:
        swap_ref[...] = folded(side(own[:, :64], other[:, :64], total[:, 64:]))
    if level in (3, 4):
        next_ref[...] = rest
        send_ref[...] = folded(rest)


GRAM_OUTS = {
    3: [(64, 384), (64, 320), (160, 128)],
    4: [(64, 256), (64, 192), (96, 128)],
    5: [(64, 256), (64, 128)],
    6: [(96, 128)],
}


def gram_rows(level, first, second):
    if level == 3:
        return (side(first[:, :128], second[:, :128], first[:, 256:320]),
                side(first[:, 128:256], second[:, 128:256], first[:, 320:384]))
    if level == 4:
        return side(first[:, :128], second[:, :128]), side(first[:, 128:], second[:, 128:])
    if level == 5:
        return side(first[:, :64], second[:, :128]), side(first[:, 128:192], second[:, 128:])
    return side(first[:, :64], second[:, :64]), side(first[:, 64:128], second[:, 64:128])


def solve_kernel(theirs, rhs_ref, inverse_ref, high_ref, low_ref, iterate_ref, terms_ref):
    _, core, _, _ = bits()
    half = 1 - core if theirs else core
    columns = rhs_ref[:, pl.ds(pl.multiple_of(half * 256, 256), 256)]
    iterate = mm3(split(inverse_ref[...]), split(columns), NN)
    iterate_ref[...] = iterate
    terms_ref[:, :576] = mm3(split(iterate.T), (high_ref[...], low_ref[...]), NT)
    terms_ref[:, 576:] = jnp.zeros((256, 64), F32)


def caps_kernel(caps_ref, out_ref):
    d, _, _, _ = bits()
    for level in range(LEVELS):
        cap = caps_ref[level]
        turned = stack(cap[RANK:], cap[:RANK])
        turned = side(turned[:, RANK:], turned[:, :RANK])
        out_ref[level] = either(d >> level & 1, cap, turned)


def basis_kernel(basis_ref, high_ref, low_ref):
    high_ref[...], low_ref[...] = split(basis_ref[...].T)


def solved(own, other, cap):
    keep = own.shape[1] - RANK
    return small(side(own[:, keep:], other[:, keep:]), cap, NT)


def rest_of(own, other, both, gram_own, gram_other):
    keep = own.shape[1] - RANK
    return own[:, :keep] + other[:, :keep] - small(both, stack(gram_own, gram_other), NN)


def level0_kernel(own_ref, got_ref, keep_ref, gram_ref, caps_ref, both_ref, send_ref, next_ref):
    _, _, part, _ = bits()
    own, other = own_ref[:, :576], got_ref[:, :576]
    both = solved(own, other, caps_ref[0])
    both_ref[...] = both
    rest = rest_of(own, other, both, keep_ref[128:192, :], gram_ref[128:192, :])
    send_ref[...] = either(part, rest[128:], rest[:128])
    next_ref[...] = either(part, rest[:128], rest[128:])


def level1_kernel(own_ref, got_ref, low_ref, low_got_ref, caps_ref, both_ref, send_ref, next_ref):
    _, _, _, y_high = bits()
    own, other = own_ref[...], got_ref[...]
    both = solved(own, other, caps_ref[1])
    both_ref[...] = both
    rest = rest_of(own, other, both, low_ref[:, 896:1344], low_got_ref[:, 896:1344])
    send_ref[:, :448] = either(y_high, rest[64:], rest[:64])
    next_ref[:, :448] = either(y_high, rest[:64], rest[64:])
    send_ref[:, 448:] = jnp.zeros((64, 64), F32)
    next_ref[:, 448:] = jnp.zeros((64, 64), F32)


def level2_kernel(own_ref, got_ref, low_ref, low_got_ref, caps_ref, both_ref, next_ref):
    own, other = own_ref[:, :448], got_ref[:, :448]
    both = solved(own, other, caps_ref[2])
    both_ref[...] = both
    next_ref[...] = rest_of(own, other, both, low_ref[:, 512:896], low_got_ref[:, 512:896])


def middle_kernel(level, own_ref, got_ref, swap_ref, swap_got_ref, caps_ref, both_ref, next_ref,
                  send_ref=None):
    _, core, _, _ = bits()
    own, other = own_ref[...], got_ref[...]
    if level in (4, 6):
        other = unfolded(other)
    both = solved(own, other, caps_ref[level])
    both_ref[...] = both
    mine, got = swap_ref[...], swap_got_ref[...]
    if level == 6:
        mine, got = unfolded(mine), unfolded(got)
    first, second = either(core, mine, got), either(core, got, mine)
    rest = rest_of(own, other, both, *gram_rows(level, first, second))
    if level < 6:
        next_ref[...] = rest
    else:
        next_ref[:, :128] = rest
        next_ref[:, 128:] = side(first[:, 128:], first[:, 128:])
    if level in (3, 5):
        send_ref[...] = folded(rest)


MIDDLE_OUTS = {
    3: [(64, 128), (64, 320), (160, 128)],
    4: [(64, 128), (64, 256)],
    5: [(64, 128), (64, 192), (96, 128)],
    6: [(64, 128), (64, 256)],
}


def level7_kernel(own_ref, got_ref, caps_ref, both_ref, next_ref):
    own, other = own_ref[:, :128], got_ref[:, :128]
    both = solved(own, other, caps_ref[7])
    both_ref[...] = both
    rest = rest_of(own, other, both, own_ref[:, 128:192], got_ref[:, 128:192])
    next_ref[...] = side(rest, jnp.zeros((64, RANK), F32))


def level8_kernel(own_ref, got_ref, both5_ref, both6_ref, both7_ref, caps_ref, out_ref):
    both = solved(own_ref[:, :RANK], got_ref[:, :RANK], caps_ref[8])
    out_ref[:, :128] = side(both5_ref[:, :RANK], both6_ref[:, :RANK])
    out_ref[:, 128:] = side(both7_ref[:, :RANK], both[:, :RANK])


def down2_kernel(both2_ref, both3_ref, both4_ref, out_ref):
    out_ref[:, :128] = side(both2_ref[:, RANK:], both3_ref[:, :RANK])
    out_ref[:, 128:] = both4_ref[...]


def down1_kernel(mine_ref, got_ref, both2_ref, both1_ref, out_ref):
    _, _, _, y_high = bits()
    own = side(both2_ref[:, :RANK], mine_ref[:, RANK:192])
    got = got_ref[:, :192]
    out_ref[...] = side(both1_ref[:, RANK:], either(y_high, stack(own, got), stack(got, own)))


def down0_kernel(mine_ref, got_ref, both1_ref, both0_ref, send_ref, own_ref):
    _, _, part, _ = bits()
    own = side(both1_ref[:, :RANK], mine_ref[:, RANK:])
    got = got_ref[...]
    rows = either(part, stack(own, got), stack(got, own))
    send_ref[:, :320] = side(both0_ref[:, RANK:], rows)
    own_ref[:, :320] = side(both0_ref[:, :RANK], rows)
    send_ref[:, 320:] = jnp.zeros((256, 64), F32)
    own_ref[:, 320:] = jnp.zeros((256, 64), F32)


def place(shard):
    core, part, y_high = shard >> 2, shard >> 1 & 1, shard & 1
    return y_high << 2 | (part ^ y_high) << 1 | core


def final_kernel(theirs_ref, mine_ref, got_ref, own_ref, all_ref, high_ref, low_ref, out_ref):
    _, core, _, _ = bits()
    factors = (high_ref[...], low_ref[...])
    last = [all_ref[place(shard)] for shard in range(8)]
    first, second = stack(*last[:4]), stack(*last[4:])
    own = side(own_ref[:, :320], either(core, first, second))
    other = side(got_ref[:, :320], either(core, second, first))
    own_out = mine_ref[...] - mm3(factors, split(own), NT)
    other_out = theirs_ref[...] - mm3(factors, split(other), NT)
    out_ref[:, :256] = either(core, own_out, other_out)
    out_ref[:, 256:] = either(core, other_out, own_out)


def local(rhs, leaf_inverse, basis, caps):
    partial = functools.partial
    high, low, gram_send, gram_keep = call(
        gram_kernel, [((576, 512), BF16), ((576, 512), BF16), (256, 512), (256, 512)],
        basis.T, flops=6 * 100_000_000, grant=12,
    )
    gram_got = sent(gram_send, PARTNER[0])
    iterate_theirs, terms_theirs = call(
        partial(solve_kernel, True), [(512, 256), (256, 640)],
        rhs, leaf_inverse, high, low, flops=6 * 142_000_000, grant=12,
    )
    terms_got = sent(terms_theirs, PARTNER[0])
    gram1, = call(gram_core_kernel, [(64, 1408)], gram_keep, gram_got, tokens=(terms_theirs,))
    gram1_got = sent(gram1, PARTNER[1])
    iterate_own, terms = call(
        partial(solve_kernel, False), [(512, 256), (256, 640)],
        rhs, leaf_inverse, high, low, tokens=(gram1,), flops=6 * 142_000_000, grant=12,
    )
    caps, = call(caps_kernel, [(9, 128, 128)], caps[0])
    both0, send1, state = call(
        level0_kernel, [(256, 128), (128, 512), (128, 512)],
        terms, terms_got, gram_keep, gram_got, caps,
    )
    got = sent(send1, PARTNER[1])
    gram2, = call(gram_add_kernel, [(64, 896)], gram1, gram1_got, tokens=(send1,))
    gram2_got = sent(gram2, PARTNER[2])
    both1, send2, state = call(
        level1_kernel, [(128, 128), (64, 512), (64, 512)], state, got, gram1, gram1_got, caps
    )
    got = sent(send2, PARTNER[2])
    gram, = call(gram_add_kernel, [(64, 512)], gram2, gram2_got, tokens=(send2,))
    grams = gram, sent(gram, PARTNER[3])
    both2, state = call(
        level2_kernel, [(64, 128), (64, 384)], state, got, gram2, gram2_got, caps
    )
    basis_high, basis_low = call(
        basis_kernel, [((512, 576), BF16), ((512, 576), BF16)], basis.T, tokens=(state,)
    )
    boths = []
    going = state
    for level in range(3, 7):
        got = sent(going, PARTNER[level])
        swap, *gram = call(
            partial(gram_level_kernel, level), GRAM_OUTS[level], *grams, tokens=(state,)
        )
        swap_got = sent(swap, PARTNER[0])
        if level < 6:
            grams = gram[0], sent(gram[-1], PARTNER[level + 1])
        if level == 5:
            down, = call(down2_kernel, [(64, 256)], both2, *boths)
            down_got = sent(down, PARTNER[2])
        if level == 6:
            down, = call(
                down1_kernel, [(128, 256)], down, down_got, both2, both1, tokens=(state,)
            )
            down_got = sent(down, PARTNER[1])
        both, state, *going = call(
            partial(middle_kernel, level), MIDDLE_OUTS[level],
            state, got, swap, swap_got, caps, tokens=(basis_low,) if level == 4 else (),
        )
        going = going[0] if going else state
        boths.append(both)
    got = sent(state, PARTNER[7])
    both7, state = call(level7_kernel, [(64, 128), (64, 128)], state, got, caps)
    got = sent(state, PARTNER[8])
    down_send, down_own = call(
        down0_kernel, [(256, 384), (256, 384)], down, down_got, both1, both0, tokens=(state,)
    )
    down_got = sent(down_send, PARTNER[0])
    last, = call(
        level8_kernel, [(64, 256)], state, got, *boths[2:], both7, caps, tokens=(down_own,)
    )
    octets = [list(range(n, n + 8)) for n in range(0, 512, 8)]
    gathered = lax.all_gather(last, "leaf", axis_index_groups=octets)
    out, = call(
        final_kernel, [(512, 512)], iterate_theirs, iterate_own, down_got, down_own, gathered,
        basis_high, basis_low, flops=12 * 75_000_000, grant=16,
    )
    return out


def solution(mesh):
    return jax.shard_map(
        local,
        mesh=mesh,
        in_specs=(P("leaf", None), P("leaf", None), P("leaf", None), P("leaf", None, None, None)),
        out_specs=P("leaf", None),
        check_vma=False,
    )
```

```python
import functools

import jax
import jax.numpy as jnp
from jax import lax
from jax.experimental import pallas as pl
from jax.experimental.pallas import tpu as pltpu
from jax.sharding import PartitionSpec as P

HIGHEST = lax.Precision.HIGHEST
F32 = jnp.float32
BF16 = jnp.bfloat16
RANK = 64
LEVELS = 9
PARTNER = (1, 2, 6, 8, 16, 32, 96, 128, 384)
NN, NT = ((1,), (0,)), ((1,), (1,))


def bits():
    d = lax.axis_index("leaf")
    core, y_low, y_high = d & 1, d >> 1 & 1, d >> 2 & 1
    return d, core, y_low ^ y_high, y_high


def sent(array, mask):
    count = lax.axis_size("leaf")
    return lax.ppermute(array, "leaf", [(i, i ^ mask) for i in range(count)])


def call(body, outs, *args, tokens=(), flops=0, grant=6):
    vmem = pl.BlockSpec(memory_space=pltpu.VMEM)
    shapes = [jax.ShapeDtypeStruct(o[0], o[1]) if isinstance(o[0], tuple) else
              jax.ShapeDtypeStruct(o, F32) for o in outs]
    count, after = len(args), len(args) + len(tokens)

    def kernel(*refs):
        body(*refs[:count], *refs[after:])

    moved = sum(a.size * a.dtype.itemsize for a in args)
    return pl.pallas_call(
        kernel,
        out_shape=shapes,
        in_specs=[vmem] * after,
        out_specs=[vmem] * len(outs),
        compiler_params=pltpu.CompilerParams(vmem_limit_bytes=grant * 2**20),
        cost_estimate=pl.CostEstimate(flops=flops, bytes_accessed=moved, transcendentals=0),
    )(*args, *tokens)


def mm(a, b, dims):
    return lax.dot_general(a, b, (dims, ((), ())), preferred_element_type=F32)


def split(x):
    high = x.astype(BF16)
    return high, (x - high.astype(F32)).astype(BF16)


def mm3(a, b, dims):
    return mm(a[0], b[0], dims) + (mm(a[0], b[1], dims) + mm(a[1], b[0], dims))


def small(a, b, dims):
    return lax.dot_general(a, b, (dims, ((), ())), precision=HIGHEST, preferred_element_type=F32)


def side(*parts):
    return jnp.concatenate(parts, axis=1)


def stack(*parts):
    return jnp.concatenate(parts, axis=0)


def either(flag, if_zero, if_one):
    return jnp.where(flag == 0, if_zero, if_one)


def folded(x):
    full = x.shape[1] // 128
    parts = [x[:, 128 * i : 128 * (i + 1)] for i in range(full)]
    last = x[:, 128 * full :]
    return stack(*parts, side(last[:32], last[32:]))


def unfolded(x):
    full = x.shape[0] // 64
    parts = [x[64 * i : 64 * (i + 1)] for i in range(full)]
    last = x[64 * full :]
    return side(*parts, stack(last[:, :64], last[:, 64:]))


def gram_kernel(basis_ref, high_ref, low_ref, send_ref, keep_ref):
    _, core, _, _ = bits()
    for level in range(LEVELS):
        top = (LEVELS - 1 - level) * RANK
        high, low = split(basis_ref[level * RANK : (level + 1) * RANK, :])
        high_ref[top : top + RANK, :] = high
        low_ref[top : top + RANK, :] = low

    def rows(top, bottom):
        return high_ref[top:bottom, :], low_ref[top:bottom, :]

    a = mm3(rows(320, 576), rows(0, 512), NT)
    b = mm3(rows(64, 320), rows(0, 256), NT)
    row3, row4, row5, row6, row7 = a[:64], b[192:], b[128:192], b[64:128], b[:64]
    first = side(
        row4[:, :128], side(row5[:, :64], row6[:, :64]), side(row7[:, :64], row3[:, 256:320]),
        row3[:, :128],
    )
    second = side(
        row4[:, 128:], side(row5[:, 64:128], row6[:, 64:128]), row5[:, 128:256], row3[:, 128:256]
    )
    send_ref[:192, :] = a[64:]
    keep_ref[:192, :] = a[64:]
    send_ref[192:, :] = either(core, second, first)
    keep_ref[192:, :] = either(core, first, second)


def gram_core_kernel(keep_ref, got_ref, out_ref):
    out_ref[:, :512] = keep_ref[192:, :] + got_ref[192:, :]
    out_ref[:, 512:896] = keep_ref[:64, :384] + got_ref[:64, :384]
    out_ref[:, 896:] = keep_ref[64:128, :] + got_ref[64:128, :]


def gram_add_kernel(own_ref, got_ref, out_ref):
    lanes = out_ref.shape[1]
    out_ref[...] = own_ref[:, :lanes] + got_ref[:, :lanes]


def gram_level_kernel(level, own_ref, got_ref, swap_ref, next_ref=None, send_ref=None):
    _, core, _, _ = bits()
    own, other = own_ref[...], got_ref[...]
    if level > 3:
        other = unfolded(other)
    total = own + other
    if level == 3:
        swap_ref[:, :256] = side(own[:, 384:], other[:, 384:])
        swap_ref[:, 256:] = side(own[:, 320:384], other[:, 320:384])
        rest = total[:, :320]
    elif level == 4:
        swap_ref[...] = folded(side(own[:, :128], other[:, :128], total[:, 128:192]))
        rest = total[:, 128:]
    else:
        swap_ref[:, :128] = side(other[:, :64], either(core, total[:, 128:], other[:, 128:]))
        swap_ref[:, 128:] = side(total[:, 64:128], own[:, 128:])
    if level < 5:
        next_ref[...] = rest
        send_ref[...] = folded(rest)


GRAM_OUTS = {
    3: [(64, 384), (64, 320), (160, 128)],
    4: [(160, 128), (64, 192), (96, 128)],
    5: [(64, 256)],
}


def solve_kernel(theirs, rhs_ref, inverse_ref, high_ref, low_ref, iterate_ref, terms_ref):
    _, core, _, _ = bits()
    half = 1 - core if theirs else core
    columns = rhs_ref[:, pl.ds(pl.multiple_of(half * 256, 256), 256)]
    iterate = mm3(split(inverse_ref[...]), split(columns), NN)
    iterate_ref[...] = iterate
    terms_ref[:, :576] = mm3(split(iterate.T), (high_ref[...], low_ref[...]), NT)
    terms_ref[:, 576:] = jnp.zeros((256, 64), F32)


def caps_kernel(caps_ref, out_ref):
    d, _, _, _ = bits()
    for level in range(LEVELS):
        cap = caps_ref[level]
        turned = stack(cap[RANK:], cap[:RANK])
        turned = side(turned[:, RANK:], turned[:, :RANK])
        out_ref[level] = either(d >> level & 1, cap, turned)


def basis_kernel(basis_ref, high_ref, low_ref):
    high_ref[...], low_ref[...] = split(basis_ref[...].T)


def solved(own, other, cap):
    keep = own.shape[1] - RANK
    return small(side(own[:, keep:], other[:, keep:]), cap, NT)


def rest_of(own, other, both, gram_own, gram_other):
    keep = own.shape[1] - RANK
    return own[:, :keep] + other[:, :keep] - small(both, stack(gram_own, gram_other), NN)


def level0_kernel(own_ref, got_ref, keep_ref, gram_ref, caps_ref, both_ref, send_ref, next_ref):
    _, _, part, _ = bits()
    own, other = own_ref[:, :576], got_ref[:, :576]
    both = solved(own, other, caps_ref[0])
    both_ref[...] = both
    rest = rest_of(own, other, both, keep_ref[128:192, :], gram_ref[128:192, :])
    send_ref[...] = either(part, rest[128:], rest[:128])
    next_ref[...] = either(part, rest[:128], rest[128:])


def level1_kernel(own_ref, got_ref, low_ref, low_got_ref, caps_ref, both_ref, send_ref, next_ref):
    _, _, _, y_high = bits()
    own, other = own_ref[...], got_ref[...]
    both = solved(own, other, caps_ref[1])
    both_ref[...] = both
    rest = rest_of(own, other, both, low_ref[:, 896:1344], low_got_ref[:, 896:1344])
    send_ref[:, :448] = either(y_high, rest[64:], rest[:64])
    next_ref[:, :448] = either(y_high, rest[:64], rest[64:])
    send_ref[:, 448:] = jnp.zeros((64, 64), F32)
    next_ref[:, 448:] = jnp.zeros((64, 64), F32)


def level2_kernel(own_ref, got_ref, low_ref, low_got_ref, caps_ref, both_ref, next_ref):
    own, other = own_ref[:, :448], got_ref[:, :448]
    both = solved(own, other, caps_ref[2])
    both_ref[...] = both
    next_ref[...] = rest_of(own, other, both, low_ref[:, 512:896], low_got_ref[:, 512:896])


def level3_kernel(own_ref, got_ref, swap_ref, swap_got_ref, caps_ref, both_ref, next_ref,
                  send_ref):
    _, core, _, _ = bits()
    own, other = own_ref[...], got_ref[...]
    both = solved(own, other, caps_ref[3])
    both_ref[...] = both
    mine, got = swap_ref[...], swap_got_ref[...]
    a, b = either(core, mine, got), either(core, got, mine)
    row_own = side(a[:, :128], b[:, :128], a[:, 256:320])
    row_other = side(a[:, 128:256], b[:, 128:256], a[:, 320:384])
    rest = rest_of(own, other, both, row_own, row_other)
    next_ref[...] = rest
    send_ref[...] = folded(rest)


def level4_kernel(own_ref, got_ref, swap_ref, swap_got_ref, caps_ref, both_ref, next_ref):
    _, core, _, _ = bits()
    own, other = own_ref[...], unfolded(got_ref[...])
    both = solved(own, other, caps_ref[4])
    both_ref[...] = both
    mine, got = unfolded(swap_ref[...]), unfolded(swap_got_ref[...])
    a, b = either(core, mine, got), either(core, got, mine)
    row_own = side(a[:, :128], b[:, :128])
    row_other = side(a[:, 128:256], b[:, 128:256])
    next_ref[...] = rest_of(own, other, both, row_own, row_other)


def level5_kernel(own_ref, got_ref, swap4_ref, swap4_got_ref, swap_ref, swap_got_ref, caps_ref,
                  both_ref, next_ref):
    _, core, _, _ = bits()
    own, other = own_ref[...], got_ref[...]
    both = solved(own, other, caps_ref[5])
    both_ref[...] = both
    mine, got = unfolded(swap4_ref[...]), unfolded(swap4_got_ref[...])
    a4, b4 = either(core, mine, got), either(core, got, mine)
    mine, got = swap_ref[...], swap_got_ref[...]
    a, b = either(core, mine, got), either(core, got, mine)
    row_own = side(a4[:, 256:320], b4[:, 256:320], b[:, 192:])
    row_other = side(a[:, :64], b[:, :128])
    rest = rest_of(own, other, both, row_own, row_other)
    next_ref[...] = side(rest, a[:, 128:192], b[:, 128:192], a[:, 64:128])


def level6_kernel(own_ref, got_ref, caps_ref, both_ref, next_ref):
    own, other = own_ref[:, :192], got_ref[:, :192]
    both = solved(own, other, caps_ref[6])
    both_ref[...] = both
    next_ref[:, :128] = rest_of(own, other, both, own_ref[:, 192:320], got_ref[:, 192:320])
    gram7 = own_ref[:, 320:] + got_ref[:, 320:]
    next_ref[:, 128:] = side(gram7, gram7)


def level7_kernel(own_ref, got_ref, caps_ref, both_ref, next_ref):
    own, other = own_ref[:, :128], got_ref[:, :128]
    both = solved(own, other, caps_ref[7])
    both_ref[...] = both
    rest = rest_of(own, other, both, own_ref[:, 128:192], got_ref[:, 128:192])
    next_ref[...] = side(rest, jnp.zeros((64, RANK), F32))


def level8_kernel(own_ref, got_ref, both5_ref, both6_ref, both7_ref, caps_ref, out_ref):
    both = solved(own_ref[:, :RANK], got_ref[:, :RANK], caps_ref[8])
    out_ref[:, :128] = side(both5_ref[:, :RANK], both6_ref[:, :RANK])
    out_ref[:, 128:] = side(both7_ref[:, :RANK], both[:, :RANK])


def down2_kernel(both2_ref, both3_ref, both4_ref, out_ref):
    out_ref[:, :128] = side(both2_ref[:, RANK:], both3_ref[:, :RANK])
    out_ref[:, 128:] = both4_ref[...]


def down1_kernel(mine_ref, got_ref, both2_ref, both1_ref, out_ref):
    _, _, _, y_high = bits()
    own = side(both2_ref[:, :RANK], mine_ref[:, RANK:192])
    got = got_ref[:, :192]
    out_ref[...] = side(both1_ref[:, RANK:], either(y_high, stack(own, got), stack(got, own)))


def down0_kernel(mine_ref, got_ref, both1_ref, both0_ref, send_ref, own_ref):
    _, _, part, _ = bits()
    own = side(both1_ref[:, :RANK], mine_ref[:, RANK:])
    got = got_ref[...]
    rows = either(part, stack(own, got), stack(got, own))
    send_ref[:, :320] = side(both0_ref[:, RANK:], rows)
    own_ref[:, :320] = side(both0_ref[:, :RANK], rows)
    send_ref[:, 320:] = jnp.zeros((256, 64), F32)
    own_ref[:, 320:] = jnp.zeros((256, 64), F32)


def place(shard):
    core, part, y_high = shard >> 2, shard >> 1 & 1, shard & 1
    return y_high << 2 | (part ^ y_high) << 1 | core


def final_kernel(theirs_ref, mine_ref, got_ref, own_ref, all_ref, high_ref, low_ref, out_ref):
    _, core, _, _ = bits()
    factors = (high_ref[...], low_ref[...])
    last = [all_ref[place(shard)] for shard in range(8)]
    first, second = stack(*last[:4]), stack(*last[4:])
    own = side(own_ref[:, :320], either(core, first, second))
    other = side(got_ref[:, :320], either(core, second, first))
    own_out = mine_ref[...] - mm3(factors, split(own), NT)
    other_out = theirs_ref[...] - mm3(factors, split(other), NT)
    out_ref[:, :256] = either(core, own_out, other_out)
    out_ref[:, 256:] = either(core, other_out, own_out)


def local(rhs, leaf_inverse, basis, caps):
    partial = functools.partial
    high, low, gram_send, gram_keep = call(
        gram_kernel, [((576, 512), BF16), ((576, 512), BF16), (256, 512), (256, 512)],
        basis.T, flops=6 * 100_000_000, grant=12,
    )
    gram_got = sent(gram_send, PARTNER[0])
    iterate_theirs, terms_theirs = call(
        partial(solve_kernel, True), [(512, 256), (256, 640)],
        rhs, leaf_inverse, high, low, flops=6 * 142_000_000, grant=12,
    )
    terms_got = sent(terms_theirs, PARTNER[0])
    gram1, = call(gram_core_kernel, [(64, 1408)], gram_keep, gram_got, tokens=(terms_theirs,))
    gram1_got = sent(gram1, PARTNER[1])
    iterate_own, terms = call(
        partial(solve_kernel, False), [(512, 256), (256, 640)],
        rhs, leaf_inverse, high, low, tokens=(gram1,), flops=6 * 142_000_000, grant=12,
    )
    caps, = call(caps_kernel, [(9, 128, 128)], caps[0])
    both0, send1, state = call(
        level0_kernel, [(256, 128), (128, 512), (128, 512)],
        terms, terms_got, gram_keep, gram_got, caps,
    )
    got = sent(send1, PARTNER[1])
    gram2, = call(gram_add_kernel, [(64, 896)], gram1, gram1_got, tokens=(send1,))
    gram2_got = sent(gram2, PARTNER[2])
    both1, send2, state = call(
        level1_kernel, [(128, 128), (64, 512), (64, 512)], state, got, gram1, gram1_got, caps
    )
    got = sent(send2, PARTNER[2])
    gram, = call(gram_add_kernel, [(64, 512)], gram2, gram2_got, tokens=(send2,))
    grams = gram, sent(gram, PARTNER[3])
    both2, state = call(
        level2_kernel, [(64, 128), (64, 384)], state, got, gram2, gram2_got, caps
    )
    basis_high, basis_low = call(
        basis_kernel, [((512, 576), BF16), ((512, 576), BF16)], basis.T, tokens=(state,)
    )
    got = sent(state, PARTNER[3])
    swap, gram, going = call(
        partial(gram_level_kernel, 3), GRAM_OUTS[3], *grams, tokens=(state,)
    )
    swap_got = sent(swap, PARTNER[0])
    grams = gram, sent(going, PARTNER[4])
    both3, state, going = call(
        level3_kernel, [(64, 128), (64, 320), (160, 128)], state, got, swap, swap_got, caps
    )
    got = sent(going, PARTNER[4])
    swap4, gram, going = call(
        partial(gram_level_kernel, 4), GRAM_OUTS[4], *grams, tokens=(state,)
    )
    swap4_got = sent(swap4, PARTNER[0])
    grams = gram, sent(going, PARTNER[5])
    both4, state = call(
        level4_kernel, [(64, 128), (64, 256)], state, got, swap4, swap4_got, caps,
        tokens=(basis_low,),
    )
    got = sent(state, PARTNER[5])
    swap, = call(partial(gram_level_kernel, 5), GRAM_OUTS[5], *grams, tokens=(state,))
    swap_got = sent(swap, PARTNER[0])
    both5, state = call(
        level5_kernel, [(64, 128), (64, 384)],
        state, got, swap4, swap4_got, swap, swap_got, caps,
    )
    got = sent(state, PARTNER[6])
    down, = call(down2_kernel, [(64, 256)], both2, both3, both4, tokens=(state,))
    down_got = sent(down, PARTNER[2])
    both6, state = call(level6_kernel, [(64, 128), (64, 256)], state, got, caps)
    down, = call(down1_kernel, [(128, 256)], down, down_got, both2, both1)
    down_got = sent(down, PARTNER[1])
    got = sent(state, PARTNER[7])
    both7, state = call(level7_kernel, [(64, 128), (64, 128)], state, got, caps)
    got = sent(state, PARTNER[8])
    down_send, down_own = call(
        down0_kernel, [(256, 384), (256, 384)], down, down_got, both1, both0, tokens=(state,)
    )
    down_got = sent(down_send, PARTNER[0])
    last, = call(
        level8_kernel, [(64, 256)], state, got, both5, both6, both7, caps
    )
    octets = [list(range(n, n + 8)) for n in range(0, 512, 8)]
    gathered = lax.all_gather(last, "leaf", axis_index_groups=octets)
    out, = call(
        final_kernel, [(512, 512)], iterate_theirs, iterate_own, down_got, down_own, gathered,
        basis_high, basis_low, flops=12 * 75_000_000, grant=16,
    )
    return out


def solution(mesh):
    return jax.shard_map(
        local,
        mesh=mesh,
        in_specs=(P("leaf", None), P("leaf", None), P("leaf", None), P("leaf", None, None, None)),
        out_specs=P("leaf", None),
        check_vma=False,
    )
```

```python
import functools

import jax
import jax.numpy as jnp
from jax import lax
from jax.experimental import pallas as pl
from jax.experimental.pallas import tpu as pltpu
from jax.sharding import PartitionSpec as P

HIGHEST = lax.Precision.HIGHEST
F32 = jnp.float32
BF16 = jnp.bfloat16
RANK = 64
LEVELS = 9
PARTNER = (1, 2, 6, 8, 16, 32, 96, 128, 384)
NN, NT = ((1,), (0,)), ((1,), (1,))


def bits():
    d = lax.axis_index("leaf")
    core, y_low, y_high = d & 1, d >> 1 & 1, d >> 2 & 1
    return d, core, y_low ^ y_high, y_high


def sent(array, mask):
    count = lax.axis_size("leaf")
    return lax.ppermute(array, "leaf", [(i, i ^ mask) for i in range(count)])


def call(body, outs, *args, tokens=(), flops=0, grant=6):
    vmem = pl.BlockSpec(memory_space=pltpu.VMEM)
    shapes = [jax.ShapeDtypeStruct(o[0], o[1]) if isinstance(o[0], tuple) else
              jax.ShapeDtypeStruct(o, F32) for o in outs]
    count, after = len(args), len(args) + len(tokens)

    def kernel(*refs):
        body(*refs[:count], *refs[after:])

    moved = sum(a.size * a.dtype.itemsize for a in args)
    return pl.pallas_call(
        kernel,
        out_shape=shapes,
        in_specs=[vmem] * after,
        out_specs=[vmem] * len(outs),
        compiler_params=pltpu.CompilerParams(vmem_limit_bytes=grant * 2**20),
        cost_estimate=pl.CostEstimate(flops=flops, bytes_accessed=moved, transcendentals=0),
    )(*args, *tokens)


def mm(a, b, dims):
    return lax.dot_general(a, b, (dims, ((), ())), preferred_element_type=F32)


def split(x):
    high = x.astype(BF16)
    return high, (x - high.astype(F32)).astype(BF16)


def mm3(a, b, dims):
    return mm(a[0], b[0], dims) + (mm(a[0], b[1], dims) + mm(a[1], b[0], dims))


def small(a, b, dims):
    return lax.dot_general(a, b, (dims, ((), ())), precision=HIGHEST, preferred_element_type=F32)


def side(*parts):
    return jnp.concatenate(parts, axis=1)


def stack(*parts):
    return jnp.concatenate(parts, axis=0)


def either(flag, if_zero, if_one):
    return jnp.where(flag == 0, if_zero, if_one)


def folded(x):
    full = x.shape[1] // 128
    parts = [x[:, 128 * i : 128 * (i + 1)] for i in range(full)]
    last = x[:, 128 * full :]
    return stack(*parts, side(last[:32], last[32:]))


def unfolded(x):
    full = x.shape[0] // 64
    parts = [x[64 * i : 64 * (i + 1)] for i in range(full)]
    last = x[64 * full :]
    return side(*parts, stack(last[:, :64], last[:, 64:]))


def gram_kernel(basis_ref, high_ref, low_ref, send_ref, keep_ref):
    _, core, _, _ = bits()
    for level in range(LEVELS):
        top = (LEVELS - 1 - level) * RANK
        high, low = split(basis_ref[level * RANK : (level + 1) * RANK, :])
        high_ref[top : top + RANK, :] = high
        low_ref[top : top + RANK, :] = low

    def rows(top, bottom):
        return high_ref[top:bottom, :], low_ref[top:bottom, :]

    a = mm3(rows(320, 576), rows(0, 512), NT)
    b = mm3(rows(64, 320), rows(0, 256), NT)
    row3, row4, row5, row6, row7 = a[:64], b[192:], b[128:192], b[64:128], b[:64]
    first = side(
        row4[:, :128], side(row5[:, :64], row6[:, :64]), side(row7[:, :64], row3[:, 256:320]),
        row3[:, :128],
    )
    second = side(
        row4[:, 128:], side(row5[:, 64:128], row6[:, 64:128]), row5[:, 128:256], row3[:, 128:256]
    )
    send_ref[:192, :] = a[64:]
    keep_ref[:192, :] = a[64:]
    send_ref[192:, :] = either(core, second, first)
    keep_ref[192:, :] = either(core, first, second)


def gram_core_kernel(keep_ref, got_ref, out_ref):
    out_ref[:, :512] = keep_ref[192:, :] + got_ref[192:, :]
    out_ref[:, 512:896] = keep_ref[:64, :384] + got_ref[:64, :384]
    out_ref[:, 896:] = keep_ref[64:128, :] + got_ref[64:128, :]


def gram_add_kernel(own_ref, got_ref, out_ref):
    lanes = out_ref.shape[1]
    out_ref[...] = own_ref[:, :lanes] + got_ref[:, :lanes]


def gram_level_kernel(level, own_ref, got_ref, swap_ref, next_ref=None, send_ref=None):
    _, core, _, _ = bits()
    own, other = own_ref[...], got_ref[...]
    if level > 3:
        other = unfolded(other)
    total = own + other
    if level == 3:
        swap_ref[:, :256] = side(own[:, 384:], other[:, 384:])
        swap_ref[:, 256:] = side(own[:, 320:384], other[:, 320:384])
        rest = total[:, :320]
    elif level == 4:
        swap_ref[...] = folded(side(own[:, :128], other[:, :128], total[:, 128:192]))
        rest = total[:, 128:]
    else:
        swap_ref[:, :128] = side(other[:, :64], either(core, total[:, 128:], other[:, 128:]))
        swap_ref[:, 128:] = side(total[:, 64:128], own[:, 128:])
    if level < 5:
        next_ref[...] = rest
        send_ref[...] = folded(rest)


GRAM_OUTS = {
    3: [(64, 384), (64, 320), (160, 128)],
    4: [(160, 128), (64, 192), (96, 128)],
    5: [(64, 256)],
}


def solve_kernel(theirs, rhs_ref, inverse_ref, high_ref, low_ref, iterate_ref, terms_ref):
    _, core, _, _ = bits()
    half = 1 - core if theirs else core
    columns = rhs_ref[:, pl.ds(pl.multiple_of(half * 256, 256), 256)]
    iterate = mm3(split(inverse_ref[...]), split(columns), NN)
    iterate_ref[...] = iterate
    terms_ref[:, :576] = mm3(split(iterate.T), (high_ref[...], low_ref[...]), NT)
    terms_ref[:, 576:] = jnp.zeros((256, 64), F32)


def caps_kernel(caps_ref, out_ref):
    d, _, _, _ = bits()
    for level in range(LEVELS):
        cap = caps_ref[level]
        turned = stack(cap[RANK:], cap[:RANK])
        turned = side(turned[:, RANK:], turned[:, :RANK])
        out_ref[level] = either(d >> level & 1, cap, turned)


def basis_kernel(basis_ref, high_ref, low_ref):
    high_ref[...], low_ref[...] = split(basis_ref[...].T)


def solved(own, other, cap):
    keep = own.shape[1] - RANK
    return small(side(own[:, keep:], other[:, keep:]), cap, NT)


def rest_of(own, other, both, gram_own, gram_other):
    keep = own.shape[1] - RANK
    return own[:, :keep] + other[:, :keep] - small(both, stack(gram_own, gram_other), NN)


def level0_kernel(own_ref, got_ref, keep_ref, gram_ref, caps_ref, both_ref, send_ref, next_ref):
    _, _, part, _ = bits()
    own, other = own_ref[:, :576], got_ref[:, :576]
    both = solved(own, other, caps_ref[0])
    both_ref[...] = both
    rest = rest_of(own, other, both, keep_ref[128:192, :], gram_ref[128:192, :])
    send_ref[...] = either(part, rest[128:], rest[:128])
    next_ref[...] = either(part, rest[:128], rest[128:])


def level1_kernel(own_ref, got_ref, low_ref, low_got_ref, caps_ref, both_ref, send_ref, next_ref):
    _, _, _, y_high = bits()
    own, other = own_ref[...], got_ref[...]
    both = solved(own, other, caps_ref[1])
    both_ref[...] = both
    rest = rest_of(own, other, both, low_ref[:, 896:1344], low_got_ref[:, 896:1344])
    send_ref[:, :448] = either(y_high, rest[64:], rest[:64])
    next_ref[:, :448] = either(y_high, rest[:64], rest[64:])
    send_ref[:, 448:] = jnp.zeros((64, 64), F32)
    next_ref[:, 448:] = jnp.zeros((64, 64), F32)


def level2_kernel(own_ref, got_ref, low_ref, low_got_ref, caps_ref, both_ref, next_ref):
    own, other = own_ref[:, :448], got_ref[:, :448]
    both = solved(own, other, caps_ref[2])
    both_ref[...] = both
    next_ref[...] = rest_of(own, other, both, low_ref[:, 512:896], low_got_ref[:, 512:896])


def level3_kernel(own_ref, got_ref, swap_ref, swap_got_ref, caps_ref, both_ref, next_ref,
                  send_ref):
    _, core, _, _ = bits()
    own, other = own_ref[...], got_ref[...]
    both = solved(own, other, caps_ref[3])
    both_ref[...] = both
    mine, got = swap_ref[...], swap_got_ref[...]
    a, b = either(core, mine, got), either(core, got, mine)
    row_own = side(a[:, :128], b[:, :128], a[:, 256:320])
    row_other = side(a[:, 128:256], b[:, 128:256], a[:, 320:384])
    rest = rest_of(own, other, both, row_own, row_other)
    next_ref[...] = rest
    send_ref[...] = folded(rest)


def level4_kernel(own_ref, got_ref, swap_ref, swap_got_ref, caps_ref, both_ref, next_ref):
    _, core, _, _ = bits()
    own, other = own_ref[...], unfolded(got_ref[...])
    both = solved(own, other, caps_ref[4])
    both_ref[...] = both
    mine, got = unfolded(swap_ref[...]), unfolded(swap_got_ref[...])
    a, b = either(core, mine, got), either(core, got, mine)
    row_own = side(a[:, :128], b[:, :128])
    row_other = side(a[:, 128:256], b[:, 128:256])
    next_ref[...] = rest_of(own, other, both, row_own, row_other)


def level5_kernel(own_ref, got_ref, swap4_ref, swap4_got_ref, swap_ref, swap_got_ref, caps_ref,
                  both2_ref, both3_ref, both4_ref, both_ref, next_ref, down_ref):
    down_ref[:, :128] = side(both2_ref[:, RANK:], both3_ref[:, :RANK])
    down_ref[:, 128:] = both4_ref[...]
    _, core, _, _ = bits()
    own, other = own_ref[...], got_ref[...]
    both = solved(own, other, caps_ref[5])
    both_ref[...] = both
    mine, got = unfolded(swap4_ref[...]), unfolded(swap4_got_ref[...])
    a4, b4 = either(core, mine, got), either(core, got, mine)
    mine, got = swap_ref[...], swap_got_ref[...]
    a, b = either(core, mine, got), either(core, got, mine)
    row_own = side(a4[:, 256:320], b4[:, 256:320], b[:, 192:])
    row_other = side(a[:, :64], b[:, :128])
    rest = rest_of(own, other, both, row_own, row_other)
    next_ref[...] = side(rest, a[:, 128:192], b[:, 128:192], a[:, 64:128])


def level6_kernel(own_ref, got_ref, caps_ref, down_mine_ref, down_got_ref, both2_ref, both1_ref,
                  both_ref, next_ref, down_ref):
    _, _, _, y_high = bits()
    mine = side(both2_ref[:, :RANK], down_mine_ref[:, RANK:192])
    theirs = down_got_ref[:, :192]
    rows = either(y_high, stack(mine, theirs), stack(theirs, mine))
    down_ref[...] = side(both1_ref[:, RANK:], rows)
    own, other = own_ref[:, :192], got_ref[:, :192]
    both = solved(own, other, caps_ref[6])
    both_ref[...] = both
    next_ref[:, :128] = rest_of(own, other, both, own_ref[:, 192:320], got_ref[:, 192:320])
    gram7 = own_ref[:, 320:] + got_ref[:, 320:]
    next_ref[:, 128:] = side(gram7, gram7)


def level7_kernel(own_ref, got_ref, caps_ref, both_ref, next_ref):
    own, other = own_ref[:, :128], got_ref[:, :128]
    both = solved(own, other, caps_ref[7])
    both_ref[...] = both
    rest = rest_of(own, other, both, own_ref[:, 128:192], got_ref[:, 128:192])
    next_ref[...] = side(rest, jnp.zeros((64, RANK), F32))


def level8_kernel(own_ref, got_ref, both5_ref, both6_ref, both7_ref, caps_ref, down_mine_ref,
                  down_got_ref, both1_ref, both0_ref, out_ref, down_send_ref, down_own_ref):
    _, _, part, _ = bits()
    both = solved(own_ref[:, :RANK], got_ref[:, :RANK], caps_ref[8])
    out_ref[:, :128] = side(both5_ref[:, :RANK], both6_ref[:, :RANK])
    out_ref[:, 128:] = side(both7_ref[:, :RANK], both[:, :RANK])
    mine = side(both1_ref[:, :RANK], down_mine_ref[:, RANK:])
    theirs = down_got_ref[...]
    rows = either(part, stack(mine, theirs), stack(theirs, mine))
    down_send_ref[:, :320] = side(both0_ref[:, RANK:], rows)
    down_own_ref[:, :320] = side(both0_ref[:, :RANK], rows)
    down_send_ref[:, 320:] = jnp.zeros((256, 64), F32)
    down_own_ref[:, 320:] = jnp.zeros((256, 64), F32)


def place(shard):
    core, part, y_high = shard >> 2, shard >> 1 & 1, shard & 1
    return y_high << 2 | (part ^ y_high) << 1 | core


def final_kernel(theirs_ref, mine_ref, got_ref, own_ref, all_ref, high_ref, low_ref, out_ref):
    _, core, _, _ = bits()
    factors = (high_ref[...], low_ref[...])
    last = [all_ref[place(shard)] for shard in range(8)]
    first, second = stack(*last[:4]), stack(*last[4:])
    own = side(own_ref[:, :320], either(core, first, second))
    other = side(got_ref[:, :320], either(core, second, first))
    own_out = mine_ref[...] - mm3(factors, split(own), NT)
    other_out = theirs_ref[...] - mm3(factors, split(other), NT)
    out_ref[:, :256] = either(core, own_out, other_out)
    out_ref[:, 256:] = either(core, other_out, own_out)


def local(rhs, leaf_inverse, basis, caps):
    partial = functools.partial
    high, low, gram_send, gram_keep = call(
        gram_kernel, [((576, 512), BF16), ((576, 512), BF16), (256, 512), (256, 512)],
        basis.T, flops=6 * 100_000_000, grant=12,
    )
    gram_got = sent(gram_send, PARTNER[0])
    iterate_theirs, terms_theirs = call(
        partial(solve_kernel, True), [(512, 256), (256, 640)],
        rhs, leaf_inverse, high, low, flops=6 * 142_000_000, grant=12,
    )
    terms_got = sent(terms_theirs, PARTNER[0])
    gram1, = call(gram_core_kernel, [(64, 1408)], gram_keep, gram_got, tokens=(terms_theirs,))
    gram1_got = sent(gram1, PARTNER[1])
    iterate_own, terms = call(
        partial(solve_kernel, False), [(512, 256), (256, 640)],
        rhs, leaf_inverse, high, low, tokens=(gram1,), flops=6 * 142_000_000, grant=12,
    )
    caps, = call(caps_kernel, [(9, 128, 128)], caps[0])
    both0, send1, state = call(
        level0_kernel, [(256, 128), (128, 512), (128, 512)],
        terms, terms_got, gram_keep, gram_got, caps,
    )
    got = sent(send1, PARTNER[1])
    gram2, = call(gram_add_kernel, [(64, 896)], gram1, gram1_got, tokens=(send1,))
    gram2_got = sent(gram2, PARTNER[2])
    both1, send2, state = call(
        level1_kernel, [(128, 128), (64, 512), (64, 512)], state, got, gram1, gram1_got, caps
    )
    got = sent(send2, PARTNER[2])
    gram, = call(gram_add_kernel, [(64, 512)], gram2, gram2_got, tokens=(send2,))
    grams = gram, sent(gram, PARTNER[3])
    both2, state = call(
        level2_kernel, [(64, 128), (64, 384)], state, got, gram2, gram2_got, caps
    )
    basis_high, basis_low = call(
        basis_kernel, [((512, 576), BF16), ((512, 576), BF16)], basis.T, tokens=(state,)
    )
    got = sent(state, PARTNER[3])
    swap, gram, going = call(
        partial(gram_level_kernel, 3), GRAM_OUTS[3], *grams, tokens=(state,)
    )
    swap_got = sent(swap, PARTNER[0])
    grams = gram, sent(going, PARTNER[4])
    both3, state, going = call(
        level3_kernel, [(64, 128), (64, 320), (160, 128)], state, got, swap, swap_got, caps
    )
    got = sent(going, PARTNER[4])
    swap4, gram, going = call(
        partial(gram_level_kernel, 4), GRAM_OUTS[4], *grams, tokens=(state,)
    )
    swap4_got = sent(swap4, PARTNER[0])
    grams = gram, sent(going, PARTNER[5])
    both4, state = call(
        level4_kernel, [(64, 128), (64, 256)], state, got, swap4, swap4_got, caps,
        tokens=(basis_low,),
    )
    got = sent(state, PARTNER[5])
    swap, = call(partial(gram_level_kernel, 5), GRAM_OUTS[5], *grams, tokens=(state,))
    swap_got = sent(swap, PARTNER[0])
    both5, state, down = call(
        level5_kernel, [(64, 128), (64, 384), (64, 256)],
        state, got, swap4, swap4_got, swap, swap_got, caps, both2, both3, both4,
    )
    got = sent(state, PARTNER[6])
    down_got = sent(down, PARTNER[2])
    both6, state, down = call(
        level6_kernel, [(64, 128), (64, 256), (128, 256)],
        state, got, caps, down, down_got, both2, both1,
    )
    got = sent(state, PARTNER[7])
    down_got = sent(down, PARTNER[1])
    both7, state = call(level7_kernel, [(64, 128), (64, 128)], state, got, caps)
    got = sent(state, PARTNER[8])
    last, down_send, down_own = call(
        level8_kernel, [(64, 256), (256, 384), (256, 384)],
        state, got, both5, both6, both7, caps, down, down_got, both1, both0,
    )
    down_got = sent(down_send, PARTNER[0])
    octets = [list(range(n, n + 8)) for n in range(0, 512, 8)]
    gathered = lax.all_gather(last, "leaf", axis_index_groups=octets)
    out, = call(
        final_kernel, [(512, 512)], iterate_theirs, iterate_own, down_got, down_own, gathered,
        basis_high, basis_low, flops=12 * 75_000_000, grant=16,
    )
    return out


def solution(mesh):
    return jax.shard_map(
        local,
        mesh=mesh,
        in_specs=(P("leaf", None), P("leaf", None), P("leaf", None), P("leaf", None, None, None)),
        out_specs=P("leaf", None),
        check_vma=False,
    )
```

```python
import functools

import jax
import jax.numpy as jnp
from jax import lax
from jax.experimental import pallas as pl
from jax.experimental.pallas import tpu as pltpu
from jax.sharding import PartitionSpec as P

HIGHEST = lax.Precision.HIGHEST
F32 = jnp.float32
BF16 = jnp.bfloat16
RANK = 64
LEVELS = 9
PARTNER = (1, 2, 6, 8, 16, 32, 96, 128, 384)
NN, NT = ((1,), (0,)), ((1,), (1,))


def bits():
    d = lax.axis_index("leaf")
    core, y_low, y_high = d & 1, d >> 1 & 1, d >> 2 & 1
    return d, core, y_low ^ y_high, y_high


def sent(array, mask):
    count = lax.axis_size("leaf")
    return lax.ppermute(array, "leaf", [(i, i ^ mask) for i in range(count)])


def call(body, outs, *args, tokens=(), flops=0, grant=6):
    vmem = pl.BlockSpec(memory_space=pltpu.VMEM)
    shapes = [jax.ShapeDtypeStruct(o[0], o[1]) if isinstance(o[0], tuple) else
              jax.ShapeDtypeStruct(o, F32) for o in outs]
    count, after = len(args), len(args) + len(tokens)

    def kernel(*refs):
        body(*refs[:count], *refs[after:])

    moved = sum(a.size * a.dtype.itemsize for a in args)
    return pl.pallas_call(
        kernel,
        out_shape=shapes,
        in_specs=[vmem] * after,
        out_specs=[vmem] * len(outs),
        compiler_params=pltpu.CompilerParams(vmem_limit_bytes=grant * 2**20),
        cost_estimate=pl.CostEstimate(flops=flops, bytes_accessed=moved, transcendentals=0),
    )(*args, *tokens)


def mm(a, b, dims):
    return lax.dot_general(a, b, (dims, ((), ())), preferred_element_type=F32)


def split(x):
    high = x.astype(BF16)
    return high, (x - high.astype(F32)).astype(BF16)


def mm3(a, b, dims):
    return mm(a[0], b[0], dims) + (mm(a[0], b[1], dims) + mm(a[1], b[0], dims))


def small(a, b, dims):
    return lax.dot_general(a, b, (dims, ((), ())), precision=HIGHEST, preferred_element_type=F32)


def side(*parts):
    return jnp.concatenate(parts, axis=1)


def stack(*parts):
    return jnp.concatenate(parts, axis=0)


def either(flag, if_zero, if_one):
    return jnp.where(flag == 0, if_zero, if_one)


def folded(x):
    full = x.shape[1] // 128
    parts = [x[:, 128 * i : 128 * (i + 1)] for i in range(full)]
    last = x[:, 128 * full :]
    return stack(*parts, side(last[:32], last[32:]))


def unfolded(x):
    full = x.shape[0] // 64
    parts = [x[64 * i : 64 * (i + 1)] for i in range(full)]
    last = x[64 * full :]
    return side(*parts, stack(last[:, :64], last[:, 64:]))


def gram_kernel(basis_ref, high_ref, low_ref, send_ref, keep_ref):
    _, core, _, _ = bits()
    for level in range(LEVELS):
        top = (LEVELS - 1 - level) * RANK
        high, low = split(basis_ref[level * RANK : (level + 1) * RANK, :])
        high_ref[top : top + RANK, :] = high
        low_ref[top : top + RANK, :] = low

    def rows(top, bottom):
        return high_ref[top:bottom, :], low_ref[top:bottom, :]

    a = mm3(rows(320, 576), rows(0, 512), NT)
    b = mm3(rows(64, 320), rows(0, 256), NT)
    row3, row4, row5, row6, row7 = a[:64], b[192:], b[128:192], b[64:128], b[:64]
    first = side(
        row4[:, :128], side(row5[:, :64], row6[:, :64]), side(row7[:, :64], row3[:, 256:320]),
        row3[:, :128],
    )
    second = side(
        row4[:, 128:], side(row5[:, 64:128], row6[:, 64:128]), row5[:, 128:256], row3[:, 128:256]
    )
    send_ref[:192, :] = a[64:]
    keep_ref[:192, :] = a[64:]
    send_ref[192:, :] = either(core, second, first)
    keep_ref[192:, :] = either(core, first, second)


def gram_core_kernel(keep_ref, got_ref, out_ref):
    out_ref[:, :512] = keep_ref[192:, :] + got_ref[192:, :]
    out_ref[:, 512:896] = keep_ref[:64, :384] + got_ref[:64, :384]
    out_ref[:, 896:] = keep_ref[64:128, :] + got_ref[64:128, :]


def gram_add_kernel(own_ref, got_ref, out_ref):
    lanes = out_ref.shape[1]
    out_ref[...] = own_ref[:, :lanes] + got_ref[:, :lanes]


def gram_level_kernel(level, own_ref, got_ref, swap_ref, next_ref=None, send_ref=None):
    _, core, _, _ = bits()
    own, other = own_ref[...], got_ref[...]
    if level > 3:
        other = unfolded(other)
    total = own + other
    if level == 3:
        swap_ref[:, :256] = side(own[:, 384:], other[:, 384:])
        swap_ref[:, 256:] = side(own[:, 320:384], other[:, 320:384])
        rest = total[:, :320]
    elif level == 4:
        swap_ref[...] = folded(side(own[:, :128], other[:, :128], total[:, 128:192]))
        rest = total[:, 128:]
    else:
        swap_ref[:, :128] = side(other[:, :64], either(core, total[:, 128:], other[:, 128:]))
        swap_ref[:, 128:] = side(total[:, 64:128], own[:, 128:])
    if level < 5:
        next_ref[...] = rest
        send_ref[...] = folded(rest)


GRAM_OUTS = {
    3: [(64, 384), (64, 320), (160, 128)],
    4: [(160, 128), (64, 192), (96, 128)],
    5: [(64, 256)],
}


def solve_kernel(theirs, rhs_ref, inverse_ref, high_ref, low_ref, iterate_ref, terms_ref):
    _, core, _, _ = bits()
    half = 1 - core if theirs else core
    columns = rhs_ref[:, pl.ds(pl.multiple_of(half * 256, 256), 256)]
    iterate = mm3(split(inverse_ref[...]), split(columns), NN)
    iterate_ref[...] = iterate
    terms_ref[:, :576] = mm3(split(iterate.T), (high_ref[...], low_ref[...]), NT)
    terms_ref[:, 576:] = jnp.zeros((256, 64), F32)


def caps_kernel(caps_ref, out_ref):
    d, _, _, _ = bits()
    for level in range(LEVELS):
        cap = caps_ref[level]
        turned = stack(cap[RANK:], cap[:RANK])
        turned = side(turned[:, RANK:], turned[:, :RANK])
        out_ref[level] = either(d >> level & 1, cap, turned)


def basis_kernel(basis_ref, high_ref, low_ref):
    high_ref[...], low_ref[...] = split(basis_ref[...].T)


def solved(own, other, cap):
    keep = own.shape[1] - RANK
    return small(side(own[:, keep:], other[:, keep:]), cap, NT)


def rest_of(own, other, both, gram_own, gram_other):
    keep = own.shape[1] - RANK
    return own[:, :keep] + other[:, :keep] - small(both, stack(gram_own, gram_other), NN)


def level0_kernel(own_ref, got_ref, keep_ref, gram_ref, caps_ref, both_ref, send_ref, next_ref):
    _, _, part, _ = bits()
    own, other = own_ref[:, :576], got_ref[:, :576]
    both = solved(own, other, caps_ref[0])
    both_ref[...] = both
    rest = rest_of(own, other, both, keep_ref[128:192, :], gram_ref[128:192, :])
    send_ref[...] = either(part, rest[128:], rest[:128])
    next_ref[...] = either(part, rest[:128], rest[128:])


def level1_kernel(own_ref, got_ref, low_ref, low_got_ref, caps_ref, both_ref, send_ref, next_ref):
    _, _, _, y_high = bits()
    own, other = own_ref[...], got_ref[...]
    both = solved(own, other, caps_ref[1])
    both_ref[...] = both
    rest = rest_of(own, other, both, low_ref[:, 896:1344], low_got_ref[:, 896:1344])
    send_ref[:, :448] = either(y_high, rest[64:], rest[:64])
    next_ref[:, :448] = either(y_high, rest[:64], rest[64:])
    send_ref[:, 448:] = jnp.zeros((64, 64), F32)
    next_ref[:, 448:] = jnp.zeros((64, 64), F32)


def level2_kernel(own_ref, got_ref, low_ref, low_got_ref, caps_ref, both_ref, next_ref):
    own, other = own_ref[:, :448], got_ref[:, :448]
    both = solved(own, other, caps_ref[2])
    both_ref[...] = both
    next_ref[...] = rest_of(own, other, both, low_ref[:, 512:896], low_got_ref[:, 512:896])


def level3_kernel(own_ref, got_ref, swap_ref, swap_got_ref, caps_ref, both_ref, next_ref,
                  send_ref):
    _, core, _, _ = bits()
    own, other = own_ref[...], got_ref[...]
    both = solved(own, other, caps_ref[3])
    both_ref[...] = both
    mine, got = swap_ref[...], swap_got_ref[...]
    a, b = either(core, mine, got), either(core, got, mine)
    row_own = side(a[:, :128], b[:, :128], a[:, 256:320])
    row_other = side(a[:, 128:256], b[:, 128:256], a[:, 320:384])
    rest = rest_of(own, other, both, row_own, row_other)
    next_ref[...] = rest
    send_ref[...] = folded(rest)


def level4_kernel(own_ref, got_ref, swap_ref, swap_got_ref, caps_ref, both2_ref, both_ref,
                  next_ref, down_ref):
    _, core, _, _ = bits()
    down_ref[...] = folded(both2_ref[:, RANK:])
    own, other = own_ref[...], unfolded(got_ref[...])
    both = solved(own, other, caps_ref[4])
    both_ref[...] = both
    mine, got = unfolded(swap_ref[...]), unfolded(swap_got_ref[...])
    a, b = either(core, mine, got), either(core, got, mine)
    row_own = side(a[:, :128], b[:, :128])
    row_other = side(a[:, 128:256], b[:, 128:256])
    next_ref[...] = rest_of(own, other, both, row_own, row_other)


def level5_kernel(own_ref, got_ref, swap4_ref, swap4_got_ref, swap_ref, swap_got_ref, caps_ref,
                  both2_ref, both1_ref, down_got_ref, both_ref, next_ref, down_ref):
    _, core, _, y_high = bits()
    mine, got = both2_ref[:, :RANK], unfolded(down_got_ref[...])
    down_ref[...] = side(
        both1_ref[:, RANK:], either(y_high, stack(mine, got), stack(got, mine))
    )
    own, other = own_ref[...], got_ref[...]
    both = solved(own, other, caps_ref[5])
    both_ref[...] = both
    mine, got = unfolded(swap4_ref[...]), unfolded(swap4_got_ref[...])
    a4, b4 = either(core, mine, got), either(core, got, mine)
    mine, got = swap_ref[...], swap_got_ref[...]
    a, b = either(core, mine, got), either(core, got, mine)
    row_own = side(a4[:, 256:320], b4[:, 256:320], b[:, 192:])
    row_other = side(a[:, :64], b[:, :128])
    rest = rest_of(own, other, both, row_own, row_other)
    next_ref[...] = side(rest, a[:, 128:192], b[:, 128:192], a[:, 64:128])


def level6_kernel(own_ref, got_ref, caps_ref, down_mine_ref, down_got_ref, both1_ref, both0_ref,
                  both_ref, next_ref, down_send_ref, down_own_ref):
    _, _, part, _ = bits()
    mine = side(both1_ref[:, :RANK], down_mine_ref[:, RANK:])
    theirs = down_got_ref[...]
    rows = either(part, stack(mine, theirs), stack(theirs, mine))
    fill = jnp.zeros((256, RANK), F32)
    down_send_ref[...] = side(both0_ref[:, RANK:], rows, fill)
    down_own_ref[...] = side(both0_ref[:, :RANK], rows, fill)
    own, other = own_ref[:, :192], got_ref[:, :192]
    both = solved(own, other, caps_ref[6])
    both_ref[...] = both
    next_ref[:, :128] = rest_of(own, other, both, own_ref[:, 192:320], got_ref[:, 192:320])
    gram7 = own_ref[:, 320:] + got_ref[:, 320:]
    next_ref[:, 128:] = side(gram7, gram7)


def level7_kernel(own_ref, got_ref, caps_ref, both_ref, next_ref):
    own, other = own_ref[:, :128], got_ref[:, :128]
    both = solved(own, other, caps_ref[7])
    both_ref[...] = both
    rest = rest_of(own, other, both, own_ref[:, 128:192], got_ref[:, 128:192])
    next_ref[...] = side(rest, jnp.zeros((64, RANK), F32))


def level8_kernel(own_ref, got_ref, both3_ref, both4_ref, both5_ref, both6_ref, both7_ref,
                  caps_ref, out_ref):
    both = solved(own_ref[:, :RANK], got_ref[:, :RANK], caps_ref[8])
    out_ref[:, :128] = side(both3_ref[:, :RANK], both4_ref[:, :RANK])
    out_ref[:, 128:256] = side(both5_ref[:, :RANK], both6_ref[:, :RANK])
    out_ref[:, 256:] = side(both7_ref[:, :RANK], both[:, :RANK])


def place(shard):
    core, part, y_high = shard >> 2, shard >> 1 & 1, shard & 1
    return y_high << 2 | (part ^ y_high) << 1 | core


def final_kernel(theirs_ref, mine_ref, got_ref, own_ref, all_ref, high_ref, low_ref, out_ref):
    _, core, _, _ = bits()
    factors = (high_ref[...], low_ref[...])
    last = [all_ref[place(shard)] for shard in range(8)]
    first, second = stack(*last[:4]), stack(*last[4:])
    own = side(own_ref[:, :192], either(core, first, second))
    other = side(got_ref[:, :192], either(core, second, first))
    own_out = mine_ref[...] - mm3(factors, split(own), NT)
    other_out = theirs_ref[...] - mm3(factors, split(other), NT)
    out_ref[:, :256] = either(core, own_out, other_out)
    out_ref[:, 256:] = either(core, other_out, own_out)


def local(rhs, leaf_inverse, basis, caps):
    partial = functools.partial
    high, low, gram_send, gram_keep = call(
        gram_kernel, [((576, 512), BF16), ((576, 512), BF16), (256, 512), (256, 512)],
        basis.T, flops=6 * 100_000_000, grant=12,
    )
    gram_got = sent(gram_send, PARTNER[0])
    iterate_theirs, terms_theirs = call(
        partial(solve_kernel, True), [(512, 256), (256, 640)],
        rhs, leaf_inverse, high, low, flops=6 * 142_000_000, grant=12,
    )
    terms_got = sent(terms_theirs, PARTNER[0])
    gram1, = call(gram_core_kernel, [(64, 1408)], gram_keep, gram_got, tokens=(terms_theirs,))
    gram1_got = sent(gram1, PARTNER[1])
    iterate_own, terms = call(
        partial(solve_kernel, False), [(512, 256), (256, 640)],
        rhs, leaf_inverse, high, low, tokens=(gram1,), flops=6 * 142_000_000, grant=12,
    )
    caps, = call(caps_kernel, [(9, 128, 128)], caps[0])
    both0, send1, state = call(
        level0_kernel, [(256, 128), (128, 512), (128, 512)],
        terms, terms_got, gram_keep, gram_got, caps,
    )
    got = sent(send1, PARTNER[1])
    gram2, = call(gram_add_kernel, [(64, 896)], gram1, gram1_got, tokens=(send1,))
    gram2_got = sent(gram2, PARTNER[2])
    both1, send2, state = call(
        level1_kernel, [(128, 128), (64, 512), (64, 512)], state, got, gram1, gram1_got, caps
    )
    got = sent(send2, PARTNER[2])
    gram, = call(gram_add_kernel, [(64, 512)], gram2, gram2_got, tokens=(send2,))
    grams = gram, sent(gram, PARTNER[3])
    both2, state = call(
        level2_kernel, [(64, 128), (64, 384)], state, got, gram2, gram2_got, caps
    )
    basis_high, basis_low = call(
        basis_kernel, [((512, 576), BF16), ((512, 576), BF16)], basis.T, tokens=(state,)
    )
    got = sent(state, PARTNER[3])
    swap, gram, going = call(
        partial(gram_level_kernel, 3), GRAM_OUTS[3], *grams, tokens=(state,)
    )
    swap_got = sent(swap, PARTNER[0])
    grams = gram, sent(going, PARTNER[4])
    both3, state, going = call(
        level3_kernel, [(64, 128), (64, 320), (160, 128)], state, got, swap, swap_got, caps
    )
    got = sent(going, PARTNER[4])
    swap4, gram, going = call(
        partial(gram_level_kernel, 4), GRAM_OUTS[4], *grams, tokens=(state,)
    )
    swap4_got = sent(swap4, PARTNER[0])
    grams = gram, sent(going, PARTNER[5])
    both4, state, down = call(
        level4_kernel, [(64, 128), (64, 256), (32, 128)],
        state, got, swap4, swap4_got, caps, both2, tokens=(basis_low,),
    )
    down_got = sent(down, PARTNER[2])
    got = sent(state, PARTNER[5])
    swap, = call(partial(gram_level_kernel, 5), GRAM_OUTS[5], *grams, tokens=(state,))
    swap_got = sent(swap, PARTNER[0])
    both5, state, down = call(
        level5_kernel, [(64, 128), (64, 384), (128, 128)],
        state, got, swap4, swap4_got, swap, swap_got, caps, both2, both1, down_got,
    )
    got = sent(state, PARTNER[6])
    down_got = sent(down, PARTNER[1])
    both6, state, down_send, down_own = call(
        level6_kernel, [(64, 128), (64, 256), (256, 256), (256, 256)],
        state, got, caps, down, down_got, both1, both0,
    )
    got = sent(state, PARTNER[7])
    down_got = sent(down_send, PARTNER[0])
    both7, state = call(level7_kernel, [(64, 128), (64, 128)], state, got, caps)
    got = sent(state, PARTNER[8])
    last, = call(
        level8_kernel, [(64, 384)], state, got, both3, both4, both5, both6, both7, caps
    )
    octets = [list(range(n, n + 8)) for n in range(0, 512, 8)]
    gathered = lax.all_gather(last, "leaf", axis_index_groups=octets)
    out, = call(
        final_kernel, [(512, 512)], iterate_theirs, iterate_own, down_got, down_own, gathered,
        basis_high, basis_low, flops=12 * 75_000_000, grant=16,
    )
    return out


def solution(mesh):
    return jax.shard_map(
        local,
        mesh=mesh,
        in_specs=(P("leaf", None), P("leaf", None), P("leaf", None), P("leaf", None, None, None)),
        out_specs=P("leaf", None),
        check_vma=False,
    )
```

```python
import functools

import jax
import jax.numpy as jnp
from jax import lax
from jax.experimental import pallas as pl
from jax.experimental.pallas import tpu as pltpu
from jax.sharding import PartitionSpec as P

F32 = jnp.float32
BF16 = jnp.bfloat16
RANK = 64
LEVELS = 9
PARTNER = (1, 2, 6, 8, 16, 32, 96, 128, 384)
NN, NT = ((1,), (0,)), ((1,), (1,))


def bits():
    d = lax.axis_index("leaf")
    core, y_low, y_high = d & 1, d >> 1 & 1, d >> 2 & 1
    return d, core, y_low ^ y_high, y_high


def sent(array, mask):
    count = lax.axis_size("leaf")
    return lax.ppermute(array, "leaf", [(i, i ^ mask) for i in range(count)])


def call(body, outs, *args, tokens=(), flops=0, grant=6):
    vmem = pl.BlockSpec(memory_space=pltpu.VMEM)
    shapes = [jax.ShapeDtypeStruct(o[0], o[1]) if isinstance(o[0], tuple) else
              jax.ShapeDtypeStruct(o, F32) for o in outs]
    count, after = len(args), len(args) + len(tokens)

    def kernel(*refs):
        body(*refs[:count], *refs[after:])

    moved = sum(a.size * a.dtype.itemsize for a in args)
    return pl.pallas_call(
        kernel,
        out_shape=shapes,
        in_specs=[vmem] * after,
        out_specs=[vmem] * len(outs),
        compiler_params=pltpu.CompilerParams(vmem_limit_bytes=grant * 2**20),
        cost_estimate=pl.CostEstimate(flops=flops, bytes_accessed=moved, transcendentals=0),
    )(*args, *tokens)


def mm(a, b, dims):
    return lax.dot_general(a, b, (dims, ((), ())), preferred_element_type=F32)


def split(x):
    high = x.astype(BF16)
    return high, (x - high.astype(F32)).astype(BF16)


def mm3(a, b, dims):
    return mm(a[0], b[0], dims) + (mm(a[0], b[1], dims) + mm(a[1], b[0], dims))


def small(a, b, dims):
    return mm3(split(a), split(b), dims)


def side(*parts):
    return jnp.concatenate(parts, axis=1)


def stack(*parts):
    return jnp.concatenate(parts, axis=0)


def either(flag, if_zero, if_one):
    return jnp.where(flag == 0, if_zero, if_one)


def folded(x):
    full = x.shape[1] // 128
    parts = [x[:, 128 * i : 128 * (i + 1)] for i in range(full)]
    last = x[:, 128 * full :]
    return stack(*parts, side(last[:32], last[32:]))


def unfolded(x):
    full = x.shape[0] // 64
    parts = [x[64 * i : 64 * (i + 1)] for i in range(full)]
    last = x[64 * full :]
    return side(*parts, stack(last[:, :64], last[:, 64:]))


def gram_kernel(basis_ref, high_ref, low_ref, send_ref, keep_ref):
    _, core, _, _ = bits()
    for level in range(LEVELS):
        top = (LEVELS - 1 - level) * RANK
        high, low = split(basis_ref[level * RANK : (level + 1) * RANK, :])
        high_ref[top : top + RANK, :] = high
        low_ref[top : top + RANK, :] = low

    def rows(top, bottom):
        return high_ref[top:bottom, :], low_ref[top:bottom, :]

    a = mm3(rows(320, 576), rows(0, 512), NT)
    b = mm3(rows(64, 320), rows(0, 256), NT)
    row3, row4, row5, row6, row7 = a[:64], b[192:], b[128:192], b[64:128], b[:64]
    first = side(
        row4[:, :128], side(row5[:, :64], row6[:, :64]), side(row7[:, :64], row3[:, 256:320]),
        row3[:, :128],
    )
    second = side(
        row4[:, 128:], side(row5[:, 64:128], row6[:, 64:128]), row5[:, 128:256], row3[:, 128:256]
    )
    send_ref[:192, :] = a[64:]
    keep_ref[:192, :] = a[64:]
    send_ref[192:, :] = either(core, second, first)
    keep_ref[192:, :] = either(core, first, second)


def gram_core_kernel(keep_ref, got_ref, out_ref):
    out_ref[:, :512] = keep_ref[192:, :] + got_ref[192:, :]
    out_ref[:, 512:896] = keep_ref[:64, :384] + got_ref[:64, :384]
    out_ref[:, 896:] = keep_ref[64:128, :] + got_ref[64:128, :]


def gram_add_kernel(own_ref, got_ref, out_ref):
    lanes = out_ref.shape[1]
    out_ref[...] = own_ref[:, :lanes] + got_ref[:, :lanes]


def gram_level_kernel(level, own_ref, got_ref, swap_ref, next_ref=None, send_ref=None):
    _, core, _, _ = bits()
    own, other = own_ref[...], got_ref[...]
    if level > 3:
        other = unfolded(other)
    total = own + other
    if level == 3:
        swap_ref[:, :256] = side(own[:, 384:], other[:, 384:])
        swap_ref[:, 256:] = side(own[:, 320:384], other[:, 320:384])
        rest = total[:, :320]
    elif level == 4:
        swap_ref[...] = folded(side(own[:, :128], other[:, :128], total[:, 128:192]))
        rest = total[:, 128:]
    else:
        swap_ref[:, :128] = side(other[:, :64], either(core, total[:, 128:], other[:, 128:]))
        swap_ref[:, 128:] = side(total[:, 64:128], own[:, 128:])
    if level < 5:
        next_ref[...] = rest
        send_ref[...] = folded(rest)


GRAM_OUTS = {
    3: [(64, 384), (64, 320), (160, 128)],
    4: [(160, 128), (64, 192), (96, 128)],
    5: [(64, 256)],
}


def solve_kernel(theirs, rhs_ref, inverse_ref, high_ref, low_ref, iterate_ref, terms_ref):
    _, core, _, _ = bits()
    half = 1 - core if theirs else core
    columns = rhs_ref[:, pl.ds(pl.multiple_of(half * 256, 256), 256)]
    iterate = mm3(split(inverse_ref[...]), split(columns), NN)
    iterate_ref[...] = iterate
    terms_ref[:, :576] = mm3(split(iterate.T), (high_ref[...], low_ref[...]), NT)
    terms_ref[:, 576:] = jnp.zeros((256, 64), F32)


def caps_kernel(caps_ref, out_ref):
    d, _, _, _ = bits()
    for level in range(LEVELS):
        cap = caps_ref[level]
        turned = stack(cap[RANK:], cap[:RANK])
        turned = side(turned[:, RANK:], turned[:, :RANK])
        out_ref[level] = either(d >> level & 1, cap, turned)


def basis_kernel(basis_ref, high_ref, low_ref):
    high_ref[...], low_ref[...] = split(basis_ref[...].T)


def solved(own, other, cap):
    keep = own.shape[1] - RANK
    return small(side(own[:, keep:], other[:, keep:]), cap, NT)


def rest_of(own, other, both, gram_own, gram_other):
    keep = own.shape[1] - RANK
    return own[:, :keep] + other[:, :keep] - small(both, stack(gram_own, gram_other), NN)


def level0_kernel(own_ref, got_ref, keep_ref, gram_ref, caps_ref, both_ref, send_ref, next_ref):
    _, _, part, _ = bits()
    own, other = own_ref[:, :576], got_ref[:, :576]
    both = solved(own, other, caps_ref[0])
    both_ref[...] = both
    rest = rest_of(own, other, both, keep_ref[128:192, :], gram_ref[128:192, :])
    send_ref[...] = either(part, rest[128:], rest[:128])
    next_ref[...] = either(part, rest[:128], rest[128:])


def level1_kernel(own_ref, got_ref, low_ref, low_got_ref, caps_ref, both_ref, send_ref, next_ref):
    _, _, _, y_high = bits()
    own, other = own_ref[...], got_ref[...]
    both = solved(own, other, caps_ref[1])
    both_ref[...] = both
    rest = rest_of(own, other, both, low_ref[:, 896:1344], low_got_ref[:, 896:1344])
    send_ref[:, :448] = either(y_high, rest[64:], rest[:64])
    next_ref[:, :448] = either(y_high, rest[:64], rest[64:])
    send_ref[:, 448:] = jnp.zeros((64, 64), F32)
    next_ref[:, 448:] = jnp.zeros((64, 64), F32)


def level2_kernel(own_ref, got_ref, low_ref, low_got_ref, caps_ref, both_ref, next_ref):
    own, other = own_ref[:, :448], got_ref[:, :448]
    both = solved(own, other, caps_ref[2])
    both_ref[...] = both
    next_ref[...] = rest_of(own, other, both, low_ref[:, 512:896], low_got_ref[:, 512:896])


def level3_kernel(own_ref, got_ref, swap_ref, swap_got_ref, caps_ref, both_ref, next_ref,
                  send_ref):
    _, core, _, _ = bits()
    own, other = own_ref[...], got_ref[...]
    both = solved(own, other, caps_ref[3])
    both_ref[...] = both
    mine, got = swap_ref[...], swap_got_ref[...]
    a, b = either(core, mine, got), either(core, got, mine)
    row_own = side(a[:, :128], b[:, :128], a[:, 256:320])
    row_other = side(a[:, 128:256], b[:, 128:256], a[:, 320:384])
    rest = rest_of(own, other, both, row_own, row_other)
    next_ref[...] = rest
    send_ref[...] = folded(rest)


def level4_kernel(own_ref, got_ref, swap_ref, swap_got_ref, caps_ref, both2_ref, both_ref,
                  next_ref, down_ref):
    _, core, _, _ = bits()
    down_ref[...] = folded(both2_ref[:, RANK:])
    own, other = own_ref[...], unfolded(got_ref[...])
    both = solved(own, other, caps_ref[4])
    both_ref[...] = both
    mine, got = unfolded(swap_ref[...]), unfolded(swap_got_ref[...])
    a, b = either(core, mine, got), either(core, got, mine)
    row_own = side(a[:, :128], b[:, :128])
    row_other = side(a[:, 128:256], b[:, 128:256])
    next_ref[...] = rest_of(own, other, both, row_own, row_other)


def level5_kernel(own_ref, got_ref, swap4_ref, swap4_got_ref, swap_ref, swap_got_ref, caps_ref,
                  both2_ref, both1_ref, down_got_ref, both_ref, next_ref, down_ref):
    _, core, _, y_high = bits()
    mine, got = both2_ref[:, :RANK], unfolded(down_got_ref[...])
    down_ref[...] = side(
        both1_ref[:, RANK:], either(y_high, stack(mine, got), stack(got, mine))
    )
    own, other = own_ref[...], got_ref[...]
    both = solved(own, other, caps_ref[5])
    both_ref[...] = both
    mine, got = unfolded(swap4_ref[...]), unfolded(swap4_got_ref[...])
    a4, b4 = either(core, mine, got), either(core, got, mine)
    mine, got = swap_ref[...], swap_got_ref[...]
    a, b = either(core, mine, got), either(core, got, mine)
    row_own = side(a4[:, 256:320], b4[:, 256:320], b[:, 192:])
    row_other = side(a[:, :64], b[:, :128])
    rest = rest_of(own, other, both, row_own, row_other)
    next_ref[...] = side(rest, a[:, 128:192], b[:, 128:192], a[:, 64:128])


def level6_kernel(own_ref, got_ref, caps_ref, down_mine_ref, down_got_ref, both1_ref, both0_ref,
                  both_ref, next_ref, down_send_ref, down_own_ref):
    _, _, part, _ = bits()
    mine = side(both1_ref[:, :RANK], down_mine_ref[:, RANK:])
    theirs = down_got_ref[...]
    rows = either(part, stack(mine, theirs), stack(theirs, mine))
    fill = jnp.zeros((256, RANK), F32)
    down_send_ref[...] = side(both0_ref[:, RANK:], rows, fill)
    down_own_ref[...] = side(both0_ref[:, :RANK], rows, fill)
    own, other = own_ref[:, :192], got_ref[:, :192]
    both = solved(own, other, caps_ref[6])
    both_ref[...] = both
    next_ref[:, :128] = rest_of(own, other, both, own_ref[:, 192:320], got_ref[:, 192:320])
    gram7 = own_ref[:, 320:] + got_ref[:, 320:]
    next_ref[:, 128:] = side(gram7, gram7)


def level7_kernel(own_ref, got_ref, caps_ref, both_ref, next_ref):
    own, other = own_ref[:, :128], got_ref[:, :128]
    both = solved(own, other, caps_ref[7])
    both_ref[...] = both
    rest = rest_of(own, other, both, own_ref[:, 128:192], got_ref[:, 128:192])
    next_ref[...] = side(rest, jnp.zeros((64, RANK), F32))


def level8_kernel(own_ref, got_ref, both3_ref, both4_ref, both5_ref, both6_ref, both7_ref,
                  caps_ref, out_ref):
    both = solved(own_ref[:, :RANK], got_ref[:, :RANK], caps_ref[8])
    out_ref[:, :128] = side(both3_ref[:, :RANK], both4_ref[:, :RANK])
    out_ref[:, 128:256] = side(both5_ref[:, :RANK], both6_ref[:, :RANK])
    out_ref[:, 256:] = side(both7_ref[:, :RANK], both[:, :RANK])


def place(shard):
    core, part, y_high = shard >> 2, shard >> 1 & 1, shard & 1
    return y_high << 2 | (part ^ y_high) << 1 | core


def final_kernel(theirs_ref, mine_ref, got_ref, own_ref, all_ref, high_ref, low_ref, out_ref):
    _, core, _, _ = bits()
    factors = (high_ref[...], low_ref[...])
    last = [all_ref[place(shard)] for shard in range(8)]
    first, second = stack(*last[:4]), stack(*last[4:])
    own = side(own_ref[:, :192], either(core, first, second))
    other = side(got_ref[:, :192], either(core, second, first))
    own_out = mine_ref[...] - mm3(factors, split(own), NT)
    other_out = theirs_ref[...] - mm3(factors, split(other), NT)
    out_ref[:, :256] = either(core, own_out, other_out)
    out_ref[:, 256:] = either(core, other_out, own_out)


def local(rhs, leaf_inverse, basis, caps):
    partial = functools.partial
    high, low, gram_send, gram_keep = call(
        gram_kernel, [((576, 512), BF16), ((576, 512), BF16), (256, 512), (256, 512)],
        basis.T, flops=6 * 100_000_000, grant=12,
    )
    gram_got = sent(gram_send, PARTNER[0])
    iterate_theirs, terms_theirs = call(
        partial(solve_kernel, True), [(512, 256), (256, 640)],
        rhs, leaf_inverse, high, low, flops=6 * 142_000_000, grant=12,
    )
    terms_got = sent(terms_theirs, PARTNER[0])
    gram1, = call(gram_core_kernel, [(64, 1408)], gram_keep, gram_got, tokens=(terms_theirs,))
    gram1_got = sent(gram1, PARTNER[1])
    iterate_own, terms = call(
        partial(solve_kernel, False), [(512, 256), (256, 640)],
        rhs, leaf_inverse, high, low, tokens=(gram1,), flops=6 * 142_000_000, grant=12,
    )
    caps, = call(caps_kernel, [(9, 128, 128)], caps[0])
    both0, send1, state = call(
        level0_kernel, [(256, 128), (128, 512), (128, 512)],
        terms, terms_got, gram_keep, gram_got, caps,
    )
    got = sent(send1, PARTNER[1])
    gram2, = call(gram_add_kernel, [(64, 896)], gram1, gram1_got, tokens=(send1,))
    gram2_got = sent(gram2, PARTNER[2])
    both1, send2, state = call(
        level1_kernel, [(128, 128), (64, 512), (64, 512)], state, got, gram1, gram1_got, caps
    )
    got = sent(send2, PARTNER[2])
    gram, = call(gram_add_kernel, [(64, 512)], gram2, gram2_got, tokens=(send2,))
    grams = gram, sent(gram, PARTNER[3])
    both2, state = call(
        level2_kernel, [(64, 128), (64, 384)], state, got, gram2, gram2_got, caps
    )
    basis_high, basis_low = call(
        basis_kernel, [((512, 576), BF16), ((512, 576), BF16)], basis.T, tokens=(state,)
    )
    got = sent(state, PARTNER[3])
    swap, gram, going = call(
        partial(gram_level_kernel, 3), GRAM_OUTS[3], *grams, tokens=(state,)
    )
    swap_got = sent(swap, PARTNER[0])
    grams = gram, sent(going, PARTNER[4])
    both3, state, going = call(
        level3_kernel, [(64, 128), (64, 320), (160, 128)], state, got, swap, swap_got, caps
    )
    got = sent(going, PARTNER[4])
    swap4, gram, going = call(
        partial(gram_level_kernel, 4), GRAM_OUTS[4], *grams, tokens=(state,)
    )
    swap4_got = sent(swap4, PARTNER[0])
    grams = gram, sent(going, PARTNER[5])
    both4, state, down = call(
        level4_kernel, [(64, 128), (64, 256), (32, 128)],
        state, got, swap4, swap4_got, caps, both2, tokens=(basis_low,),
    )
    down_got = sent(down, PARTNER[2])
    got = sent(state, PARTNER[5])
    swap, = call(partial(gram_level_kernel, 5), GRAM_OUTS[5], *grams, tokens=(state,))
    swap_got = sent(swap, PARTNER[0])
    both5, state, down = call(
        level5_kernel, [(64, 128), (64, 384), (128, 128)],
        state, got, swap4, swap4_got, swap, swap_got, caps, both2, both1, down_got,
    )
    got = sent(state, PARTNER[6])
    down_got = sent(down, PARTNER[1])
    both6, state, down_send, down_own = call(
        level6_kernel, [(64, 128), (64, 256), (256, 256), (256, 256)],
        state, got, caps, down, down_got, both1, both0,
    )
    got = sent(state, PARTNER[7])
    down_got = sent(down_send, PARTNER[0])
    both7, state = call(level7_kernel, [(64, 128), (64, 128)], state, got, caps)
    got = sent(state, PARTNER[8])
    last, = call(
        level8_kernel, [(64, 384)], state, got, both3, both4, both5, both6, both7, caps
    )
    octets = [list(range(n, n + 8)) for n in range(0, 512, 8)]
    gathered = lax.all_gather(last, "leaf", axis_index_groups=octets)
    out, = call(
        final_kernel, [(512, 512)], iterate_theirs, iterate_own, down_got, down_own, gathered,
        basis_high, basis_low, flops=12 * 75_000_000, grant=16,
    )
    return out


def solution(mesh):
    return jax.shard_map(
        local,
        mesh=mesh,
        in_specs=(P("leaf", None), P("leaf", None), P("leaf", None), P("leaf", None, None, None)),
        out_specs=P("leaf", None),
        check_vma=False,
    )
```

```python
import functools

import jax
import jax.numpy as jnp
from jax import lax
from jax.experimental import pallas as pl
from jax.experimental.pallas import tpu as pltpu
from jax.sharding import PartitionSpec as P

F32 = jnp.float32
BF16 = jnp.bfloat16
RANK = 64
LEVELS = 9
PARTNER = (1, 2, 6, 8, 16, 32, 96, 128, 384)
NN, NT = ((1,), (0,)), ((1,), (1,))


def bits():
    d = lax.axis_index("leaf")
    core, y_low, y_high = d & 1, d >> 1 & 1, d >> 2 & 1
    return d, core, y_low ^ y_high, y_high


def sent(array, mask):
    count = lax.axis_size("leaf")
    return lax.ppermute(array, "leaf", [(i, i ^ mask) for i in range(count)])


def call(body, outs, *args, tokens=(), flops=0, grant=6):
    vmem = pl.BlockSpec(memory_space=pltpu.VMEM)
    shapes = [jax.ShapeDtypeStruct(o[0], o[1]) if isinstance(o[0], tuple) else
              jax.ShapeDtypeStruct(o, F32) for o in outs]
    count, after = len(args), len(args) + len(tokens)

    def kernel(*refs):
        body(*refs[:count], *refs[after:])

    moved = sum(a.size * a.dtype.itemsize for a in args)
    return pl.pallas_call(
        kernel,
        out_shape=shapes,
        in_specs=[vmem] * after,
        out_specs=[vmem] * len(outs),
        compiler_params=pltpu.CompilerParams(vmem_limit_bytes=grant * 2**20),
        cost_estimate=pl.CostEstimate(flops=flops, bytes_accessed=moved, transcendentals=0),
    )(*args, *tokens)


def mm(a, b, dims):
    return lax.dot_general(a, b, (dims, ((), ())), preferred_element_type=F32)


def split(x):
    high = x.astype(BF16)
    return high, (x - high.astype(F32)).astype(BF16)


def mm3(a, b, dims):
    return mm(a[0], b[0], dims) + (mm(a[0], b[1], dims) + mm(a[1], b[0], dims))


def small(a, b, dims):
    return mm3(split(a), split(b), dims)


def side(*parts):
    return jnp.concatenate(parts, axis=1)


def stack(*parts):
    return jnp.concatenate(parts, axis=0)


def either(flag, if_zero, if_one):
    return jnp.where(flag == 0, if_zero, if_one)


def folded(x):
    full = x.shape[1] // 128
    parts = [x[:, 128 * i : 128 * (i + 1)] for i in range(full)]
    last = x[:, 128 * full :]
    return stack(*parts, side(last[:32], last[32:]))


def unfolded(x):
    full = x.shape[0] // 64
    parts = [x[64 * i : 64 * (i + 1)] for i in range(full)]
    last = x[64 * full :]
    return side(*parts, stack(last[:, :64], last[:, 64:]))


def gram_kernel(basis_ref, high_ref, low_ref, send_ref, keep_ref):
    _, core, _, _ = bits()
    for level in range(LEVELS):
        top = (LEVELS - 1 - level) * RANK
        high, low = split(basis_ref[level * RANK : (level + 1) * RANK, :])
        high_ref[top : top + RANK, :] = high
        low_ref[top : top + RANK, :] = low

    def rows(top, bottom):
        return high_ref[top:bottom, :], low_ref[top:bottom, :]

    a = mm3(rows(320, 576), rows(0, 512), NT)
    b = mm3(rows(64, 320), rows(0, 256), NT)
    row3, row4, row5, row6, row7 = a[:64], b[192:], b[128:192], b[64:128], b[:64]
    first = side(
        row4[:, :128], side(row5[:, :64], row6[:, :64]), side(row7[:, :64], row3[:, 256:320]),
        row3[:, :128],
    )
    second = side(
        row4[:, 128:], side(row5[:, 64:128], row6[:, 64:128]), row5[:, 128:256], row3[:, 128:256]
    )
    send_ref[:192, :] = a[64:]
    keep_ref[:192, :] = a[64:]
    send_ref[192:, :] = either(core, second, first)
    keep_ref[192:, :] = either(core, first, second)


def gram_core_kernel(keep_ref, got_ref, out_ref):
    out_ref[...] = folded(side(
        keep_ref[192:, :] + got_ref[192:, :],
        keep_ref[:64, :384] + got_ref[:64, :384],
        keep_ref[64:128, :448] + got_ref[64:128, :448],
    ))


def gram_y_kernel(own_ref, got_ref, out_ref):
    out_ref[...] = unfolded(own_ref[...] + got_ref[...])[:, :896]


def gram_add_kernel(own_ref, got_ref, out_ref):
    lanes = out_ref.shape[1]
    out_ref[...] = own_ref[:, :lanes] + got_ref[:, :lanes]


def gram_level_kernel(level, own_ref, got_ref, swap_ref, next_ref=None, send_ref=None):
    _, core, _, _ = bits()
    own, other = own_ref[...], got_ref[...]
    if level > 3:
        other = unfolded(other)
    total = own + other
    if level == 3:
        swap_ref[:, :256] = side(own[:, 384:], other[:, 384:])
        swap_ref[:, 256:] = side(own[:, 320:384], other[:, 320:384])
        rest = total[:, :320]
    elif level == 4:
        swap_ref[...] = folded(side(own[:, :128], other[:, :128], total[:, 128:192]))
        rest = total[:, 128:]
    else:
        swap_ref[:, :128] = side(other[:, :64], either(core, total[:, 128:], other[:, 128:]))
        swap_ref[:, 128:] = side(total[:, 64:128], own[:, 128:])
    if level < 5:
        next_ref[...] = rest
        send_ref[...] = folded(rest)


GRAM_OUTS = {
    3: [(64, 384), (64, 320), (160, 128)],
    4: [(160, 128), (64, 192), (96, 128)],
    5: [(64, 256)],
}


def solve_kernel(theirs, rhs_ref, inverse_ref, high_ref, low_ref, iterate_ref, terms_ref):
    _, core, _, _ = bits()
    half = 1 - core if theirs else core
    columns = rhs_ref[:, pl.ds(pl.multiple_of(half * 256, 256), 256)]
    iterate = mm3(split(inverse_ref[...]), split(columns), NN)
    iterate_ref[...] = iterate
    terms_ref[:, :576] = mm3(split(iterate.T), (high_ref[...], low_ref[...]), NT)
    terms_ref[:, 576:] = jnp.zeros((256, 64), F32)


def caps_kernel(caps_ref, out_ref):
    d, _, _, _ = bits()
    for level in range(LEVELS):
        cap = caps_ref[level]
        turned = stack(cap[RANK:], cap[:RANK])
        turned = side(turned[:, RANK:], turned[:, :RANK])
        out_ref[level] = either(d >> level & 1, cap, turned)


def basis_kernel(basis_ref, high_ref, low_ref):
    high_ref[...], low_ref[...] = split(basis_ref[...].T)


def solved(own, other, cap):
    keep = own.shape[1] - RANK
    return small(side(own[:, keep:], other[:, keep:]), cap, NT)


def rest_of(own, other, both, gram_own, gram_other):
    keep = own.shape[1] - RANK
    return own[:, :keep] + other[:, :keep] - small(both, stack(gram_own, gram_other), NN)


def level0_kernel(own_ref, got_ref, keep_ref, gram_ref, caps_ref, both_ref, send_ref, next_ref):
    _, _, part, _ = bits()
    own, other = own_ref[:, :576], got_ref[:, :576]
    both = solved(own, other, caps_ref[0])
    both_ref[...] = both
    rest = rest_of(own, other, both, keep_ref[128:192, :], gram_ref[128:192, :])
    send_ref[...] = either(part, rest[128:], rest[:128])
    next_ref[...] = either(part, rest[:128], rest[128:])


def level1_kernel(own_ref, got_ref, low_ref, low_got_ref, caps_ref, both_ref, send_ref, next_ref):
    _, _, _, y_high = bits()
    own, other = own_ref[...], got_ref[...]
    both = solved(own, other, caps_ref[1])
    both_ref[...] = both
    rest = rest_of(own, other, both, unfolded(low_ref[...])[:, 896:], unfolded(low_got_ref[...])[:, 896:])
    send_ref[:, :448] = either(y_high, rest[64:], rest[:64])
    next_ref[:, :448] = either(y_high, rest[:64], rest[64:])
    send_ref[:, 448:] = jnp.zeros((64, 64), F32)
    next_ref[:, 448:] = jnp.zeros((64, 64), F32)


def level2_kernel(own_ref, got_ref, low_ref, low_got_ref, caps_ref, both_ref, next_ref):
    own, other = own_ref[:, :448], got_ref[:, :448]
    both = solved(own, other, caps_ref[2])
    both_ref[...] = both
    next_ref[...] = rest_of(own, other, both, low_ref[:, 512:896], low_got_ref[:, 512:896])


def level3_kernel(own_ref, got_ref, swap_ref, swap_got_ref, caps_ref, both_ref, next_ref,
                  send_ref):
    _, core, _, _ = bits()
    own, other = own_ref[...], got_ref[...]
    both = solved(own, other, caps_ref[3])
    both_ref[...] = both
    mine, got = swap_ref[...], swap_got_ref[...]
    a, b = either(core, mine, got), either(core, got, mine)
    row_own = side(a[:, :128], b[:, :128], a[:, 256:320])
    row_other = side(a[:, 128:256], b[:, 128:256], a[:, 320:384])
    rest = rest_of(own, other, both, row_own, row_other)
    next_ref[...] = rest
    send_ref[...] = folded(rest)


def level4_kernel(own_ref, got_ref, swap_ref, swap_got_ref, caps_ref, both2_ref, both_ref,
                  next_ref, down_ref):
    _, core, _, _ = bits()
    down_ref[...] = folded(both2_ref[:, RANK:])
    own, other = own_ref[...], unfolded(got_ref[...])
    both = solved(own, other, caps_ref[4])
    both_ref[...] = both
    mine, got = unfolded(swap_ref[...]), unfolded(swap_got_ref[...])
    a, b = either(core, mine, got), either(core, got, mine)
    row_own = side(a[:, :128], b[:, :128])
    row_other = side(a[:, 128:256], b[:, 128:256])
    next_ref[...] = rest_of(own, other, both, row_own, row_other)


def level5_kernel(own_ref, got_ref, swap4_ref, swap4_got_ref, swap_ref, swap_got_ref, caps_ref,
                  both2_ref, both1_ref, down_got_ref, both_ref, next_ref, down_ref):
    _, core, _, y_high = bits()
    mine, got = both2_ref[:, :RANK], unfolded(down_got_ref[...])
    down_ref[...] = side(
        both1_ref[:, RANK:], either(y_high, stack(mine, got), stack(got, mine))
    )
    own, other = own_ref[...], got_ref[...]
    both = solved(own, other, caps_ref[5])
    both_ref[...] = both
    mine, got = unfolded(swap4_ref[...]), unfolded(swap4_got_ref[...])
    a4, b4 = either(core, mine, got), either(core, got, mine)
    mine, got = swap_ref[...], swap_got_ref[...]
    a, b = either(core, mine, got), either(core, got, mine)
    row_own = side(a4[:, 256:320], b4[:, 256:320], b[:, 192:])
    row_other = side(a[:, :64], b[:, :128])
    rest = rest_of(own, other, both, row_own, row_other)
    next_ref[...] = side(rest, a[:, 128:192], b[:, 128:192], a[:, 64:128])


def level6_kernel(own_ref, got_ref, caps_ref, down_mine_ref, down_got_ref, both1_ref, both0_ref,
                  both_ref, next_ref, down_send_ref, down_own_ref):
    _, _, part, _ = bits()
    mine = side(both1_ref[:, :RANK], down_mine_ref[:, RANK:])
    theirs = down_got_ref[...]
    rows = either(part, stack(mine, theirs), stack(theirs, mine))
    fill = jnp.zeros((256, RANK), F32)
    down_send_ref[...] = side(both0_ref[:, RANK:], rows, fill)
    down_own_ref[...] = side(both0_ref[:, :RANK], rows, fill)
    own, other = own_ref[:, :192], got_ref[:, :192]
    both = solved(own, other, caps_ref[6])
    both_ref[...] = both
    rest = rest_of(own, other, both, own_ref[:, 192:320], got_ref[:, 192:320])
    next_ref[...] = folded(side(rest, own_ref[:, 320:] + got_ref[:, 320:]))


def level7_kernel(own_ref, got_ref, caps_ref, both_ref, next_ref):
    mine, theirs = unfolded(own_ref[...]), unfolded(got_ref[...])
    own, other = mine[:, :128], theirs[:, :128]
    both = solved(own, other, caps_ref[7])
    both_ref[...] = both
    next_ref[...] = folded(rest_of(own, other, both, mine[:, 128:], theirs[:, 128:]))


def level8_kernel(own_ref, got_ref, both3_ref, both4_ref, both5_ref, both6_ref, both7_ref,
                  caps_ref, out_ref):
    both = solved(unfolded(own_ref[...]), unfolded(got_ref[...]), caps_ref[8])
    out_ref[:, :128] = side(both3_ref[:, :RANK], both4_ref[:, :RANK])
    out_ref[:, 128:256] = side(both5_ref[:, :RANK], both6_ref[:, :RANK])
    out_ref[:, 256:] = side(both7_ref[:, :RANK], both[:, :RANK])


def place(shard):
    core, part, y_high = shard >> 2, shard >> 1 & 1, shard & 1
    return y_high << 2 | (part ^ y_high) << 1 | core


def final_kernel(theirs_ref, mine_ref, got_ref, own_ref, all_ref, high_ref, low_ref, out_ref,
                 block_ref, sems):
    _, core, _, _ = bits()
    last = [all_ref[place(shard)] for shard in range(8)]
    first, second = stack(*last[:4]), stack(*last[4:])
    own = split(side(own_ref[:, :192], either(core, first, second)))
    other = split(side(got_ref[:, :192], either(core, second, first)))
    copies = []
    for n in range(2):
        rows = slice(256 * n, 256 * (n + 1))
        factors = (high_ref[rows, :], low_ref[rows, :])
        own_out = mine_ref[rows, :] - mm3(factors, own, NT)
        other_out = theirs_ref[rows, :] - mm3(factors, other, NT)
        block_ref[n, :, :256] = either(core, own_out, other_out)
        block_ref[n, :, 256:] = either(core, other_out, own_out)
        copies.append(
            pltpu.make_async_copy(block_ref.at[n], out_ref.at[pl.ds(256 * n, 256)], sems.at[n])
        )
        copies[n].start()
    for copy in copies:
        copy.wait()


def final(*args):
    return pl.pallas_call(
        final_kernel,
        out_shape=jax.ShapeDtypeStruct((512, 512), F32),
        in_specs=[pl.BlockSpec(memory_space=pltpu.VMEM)] * len(args),
        out_specs=pl.BlockSpec(memory_space=pl.ANY),
        scratch_shapes=[pltpu.VMEM((2, 256, 512), F32), pltpu.SemaphoreType.DMA((2,))],
        compiler_params=pltpu.CompilerParams(vmem_limit_bytes=16 * 2**20),
        cost_estimate=pl.CostEstimate(
            flops=12 * 75_000_000, bytes_accessed=2**20, transcendentals=0
        ),
    )(*args)


def local(rhs, leaf_inverse, basis, caps):
    partial = functools.partial
    high, low, gram_send, gram_keep = call(
        gram_kernel, [((576, 512), BF16), ((576, 512), BF16), (256, 512), (256, 512)],
        basis.T, flops=6 * 100_000_000, grant=12,
    )
    gram_got = sent(gram_send, PARTNER[0])
    iterate_theirs, terms_theirs = call(
        partial(solve_kernel, True), [(512, 256), (256, 640)],
        rhs, leaf_inverse, high, low, flops=6 * 142_000_000, grant=12,
    )
    terms_got = sent(terms_theirs, PARTNER[0])
    gram1, = call(gram_core_kernel, [(672, 128)], gram_keep, gram_got, tokens=(terms_theirs,))
    gram1_got = sent(gram1, PARTNER[1])
    iterate_own, terms = call(
        partial(solve_kernel, False), [(512, 256), (256, 640)],
        rhs, leaf_inverse, high, low, tokens=(gram1,), flops=6 * 142_000_000, grant=12,
    )
    caps, = call(caps_kernel, [(9, 128, 128)], caps[0])
    both0, send1, state = call(
        level0_kernel, [(256, 128), (128, 512), (128, 512)],
        terms, terms_got, gram_keep, gram_got, caps,
    )
    got = sent(send1, PARTNER[1])
    gram2, = call(gram_y_kernel, [(64, 896)], gram1, gram1_got, tokens=(send1,))
    gram2_got = sent(gram2, PARTNER[2])
    both1, send2, state = call(
        level1_kernel, [(128, 128), (64, 512), (64, 512)], state, got, gram1, gram1_got, caps
    )
    got = sent(send2, PARTNER[2])
    gram, = call(gram_add_kernel, [(64, 512)], gram2, gram2_got, tokens=(send2,))
    grams = gram, sent(gram, PARTNER[3])
    both2, state = call(
        level2_kernel, [(64, 128), (64, 384)], state, got, gram2, gram2_got, caps
    )
    basis_high, basis_low = call(
        basis_kernel, [((512, 576), BF16), ((512, 576), BF16)], basis.T, tokens=(state,)
    )
    got = sent(state, PARTNER[3])
    swap, gram, going = call(
        partial(gram_level_kernel, 3), GRAM_OUTS[3], *grams, tokens=(state,)
    )
    swap_got = sent(swap, PARTNER[0])
    grams = gram, sent(going, PARTNER[4])
    both3, state, going = call(
        level3_kernel, [(64, 128), (64, 320), (160, 128)], state, got, swap, swap_got, caps
    )
    got = sent(going, PARTNER[4])
    swap4, gram, going = call(
        partial(gram_level_kernel, 4), GRAM_OUTS[4], *grams, tokens=(state,)
    )
    swap4_got = sent(swap4, PARTNER[0])
    grams = gram, sent(going, PARTNER[5])
    both4, state, down = call(
        level4_kernel, [(64, 128), (64, 256), (32, 128)],
        state, got, swap4, swap4_got, caps, both2, tokens=(basis_low,),
    )
    down_got = sent(down, PARTNER[2])
    got = sent(state, PARTNER[5])
    swap, = call(partial(gram_level_kernel, 5), GRAM_OUTS[5], *grams, tokens=(state,))
    swap_got = sent(swap, PARTNER[0])
    both5, state, down = call(
        level5_kernel, [(64, 128), (64, 384), (128, 128)],
        state, got, swap4, swap4_got, swap, swap_got, caps, both2, both1, down_got,
    )
    got = sent(state, PARTNER[6])
    down_got = sent(down, PARTNER[1])
    both6, state, down_send, down_own = call(
        level6_kernel, [(64, 128), (96, 128), (256, 256), (256, 256)],
        state, got, caps, down, down_got, both1, both0,
    )
    got = sent(state, PARTNER[7])
    down_got = sent(down_send, PARTNER[0])
    both7, state = call(level7_kernel, [(64, 128), (32, 128)], state, got, caps)
    got = sent(state, PARTNER[8])
    last, = call(
        level8_kernel, [(64, 384)], state, got, both3, both4, both5, both6, both7, caps
    )
    octets = [list(range(n, n + 8)) for n in range(0, 512, 8)]
    gathered = lax.all_gather(last, "leaf", axis_index_groups=octets)
    return final(
        iterate_theirs, iterate_own, down_got, down_own, gathered, basis_high, basis_low
    )


def solution(mesh):
    return jax.shard_map(
        local,
        mesh=mesh,
        in_specs=(P("leaf", None), P("leaf", None), P("leaf", None), P("leaf", None, None, None)),
        out_specs=P("leaf", None),
        check_vma=False,
    )
```

```python
import functools

import jax
import jax.numpy as jnp
from jax import lax
from jax.experimental import pallas as pl
from jax.experimental.pallas import tpu as pltpu
from jax.sharding import PartitionSpec as P

F32 = jnp.float32
BF16 = jnp.bfloat16
RANK = 64
LEVELS = 9
PARTNER = (1, 2, 6, 8, 16, 32, 96, 128, 384)
NN, NT = ((1,), (0,)), ((1,), (1,))


def bits():
    d = lax.axis_index("leaf")
    core, y_low, y_high = d & 1, d >> 1 & 1, d >> 2 & 1
    return d, core, y_low ^ y_high, y_high


def sent(array, mask):
    count = lax.axis_size("leaf")
    return lax.ppermute(array, "leaf", [(i, i ^ mask) for i in range(count)])


def call(body, outs, *args, tokens=(), flops=0, grant=6):
    vmem = pl.BlockSpec(memory_space=pltpu.VMEM)
    shapes = [jax.ShapeDtypeStruct(o[0], o[1]) if isinstance(o[0], tuple) else
              jax.ShapeDtypeStruct(o, F32) for o in outs]
    count, after = len(args), len(args) + len(tokens)

    def kernel(*refs):
        body(*refs[:count], *refs[after:])

    moved = sum(a.size * a.dtype.itemsize for a in args)
    return pl.pallas_call(
        kernel,
        out_shape=shapes,
        in_specs=[vmem] * after,
        out_specs=[vmem] * len(outs),
        compiler_params=pltpu.CompilerParams(vmem_limit_bytes=grant * 2**20),
        cost_estimate=pl.CostEstimate(flops=flops, bytes_accessed=moved, transcendentals=0),
    )(*args, *tokens)


def mm(a, b, dims):
    return lax.dot_general(a, b, (dims, ((), ())), preferred_element_type=F32)


def split(x):
    high = x.astype(BF16)
    return high, (x - high.astype(F32)).astype(BF16)


def mm3(a, b, dims):
    return mm(a[0], b[0], dims) + (mm(a[0], b[1], dims) + mm(a[1], b[0], dims))


def small(a, b, dims):
    return mm3(split(a), split(b), dims)


def side(*parts):
    return jnp.concatenate(parts, axis=1)


def stack(*parts):
    return jnp.concatenate(parts, axis=0)


def either(flag, if_zero, if_one):
    return jnp.where(flag == 0, if_zero, if_one)


def folded(x):
    rows, full = x.shape[0], x.shape[1] // 128
    parts = [x[:, 128 * i : 128 * (i + 1)] for i in range(full)]
    last = x[:, 128 * full :]
    return stack(*parts, side(last[: rows // 2], last[rows // 2 :]))


def unfolded(x, rows=64):
    full = x.shape[0] // rows
    parts = [x[rows * i : rows * (i + 1)] for i in range(full)]
    last = x[rows * full :]
    return side(*parts, stack(last[:, :64], last[:, 64:]))


def gram_kernel(basis_ref, high_ref, low_ref, send_ref, keep_ref):
    _, core, _, _ = bits()
    for level in range(LEVELS):
        top = (LEVELS - 1 - level) * RANK
        high, low = split(basis_ref[level * RANK : (level + 1) * RANK, :])
        high_ref[top : top + RANK, :] = high
        low_ref[top : top + RANK, :] = low

    def rows(top, bottom):
        return high_ref[top:bottom, :], low_ref[top:bottom, :]

    a = mm3(rows(320, 576), rows(0, 512), NT)
    b = mm3(rows(64, 320), rows(0, 256), NT)
    row3, row4, row5, row6, row7 = a[:64], b[192:], b[128:192], b[64:128], b[:64]
    first = side(
        row4[:, :128], side(row5[:, :64], row6[:, :64]), side(row7[:, :64], row3[:, 256:320]),
        row3[:, :128],
    )
    second = side(
        row4[:, 128:], side(row5[:, 64:128], row6[:, 64:128]), row5[:, 128:256], row3[:, 128:256]
    )
    send_ref[:192, :] = a[64:]
    keep_ref[:192, :] = a[64:]
    send_ref[192:, :] = either(core, second, first)
    keep_ref[192:, :] = either(core, first, second)


def gram_core_kernel(keep_ref, got_ref, out_ref):
    out_ref[...] = folded(side(
        keep_ref[192:, :] + got_ref[192:, :],
        keep_ref[:64, :384] + got_ref[:64, :384],
        keep_ref[64:128, :448] + got_ref[64:128, :448],
    ))


def gram_y_kernel(own_ref, got_ref, out_ref):
    out_ref[...] = unfolded(own_ref[...] + got_ref[...])[:, :896]


def gram_add_kernel(own_ref, got_ref, out_ref):
    lanes = out_ref.shape[1]
    out_ref[...] = own_ref[:, :lanes] + got_ref[:, :lanes]


def gram_level_kernel(level, own_ref, got_ref, swap_ref, next_ref=None, send_ref=None):
    _, core, _, _ = bits()
    own, other = own_ref[...], got_ref[...]
    if level > 3:
        other = unfolded(other)
    total = own + other
    if level == 3:
        swap_ref[:, :256] = side(own[:, 384:], other[:, 384:])
        swap_ref[:, 256:] = side(own[:, 320:384], other[:, 320:384])
        rest = total[:, :320]
    elif level == 4:
        swap_ref[...] = folded(side(own[:, :128], other[:, :128], total[:, 128:192]))
        rest = total[:, 128:]
    else:
        swap_ref[:, :128] = side(other[:, :64], either(core, total[:, 128:], other[:, 128:]))
        swap_ref[:, 128:] = side(total[:, 64:128], own[:, 128:])
    if level < 5:
        next_ref[...] = rest
        send_ref[...] = folded(rest)


GRAM_OUTS = {
    3: [(64, 384), (64, 320), (160, 128)],
    4: [(160, 128), (64, 192), (96, 128)],
    5: [(64, 256)],
}


def solve_kernel(theirs, rhs_ref, inverse_ref, high_ref, low_ref, iterate_ref, terms_ref):
    _, core, _, _ = bits()
    half = 1 - core if theirs else core
    columns = rhs_ref[:, pl.ds(pl.multiple_of(half * 256, 256), 256)]
    iterate = mm3(split(inverse_ref[...]), split(columns), NN)
    iterate_ref[...] = iterate
    terms_ref[:, :576] = mm3(split(iterate.T), (high_ref[...], low_ref[...]), NT)
    terms_ref[:, 576:] = jnp.zeros((256, 64), F32)


def caps_kernel(caps_ref, out_ref):
    d, _, _, _ = bits()
    for level in range(LEVELS):
        cap = caps_ref[level]
        turned = stack(cap[RANK:], cap[:RANK])
        turned = side(turned[:, RANK:], turned[:, :RANK])
        out_ref[level] = either(d >> level & 1, cap, turned)


def basis_kernel(basis_ref, high_ref, low_ref):
    high_ref[...], low_ref[...] = split(basis_ref[...].T)


def solved(own, other, cap):
    keep = own.shape[1] - RANK
    return small(side(own[:, keep:], other[:, keep:]), cap, NT)


def rest_of(own, other, both, gram_own, gram_other):
    keep = own.shape[1] - RANK
    return own[:, :keep] + other[:, :keep] - small(both, stack(gram_own, gram_other), NN)


def level0_kernel(own_ref, got_ref, keep_ref, gram_ref, caps_ref, both_ref, send_ref, next_ref):
    _, _, part, _ = bits()
    own, other = own_ref[:, :576], got_ref[:, :576]
    both = solved(own, other, caps_ref[0])
    both_ref[...] = both
    rest = rest_of(own, other, both, keep_ref[128:192, :], gram_ref[128:192, :])
    send_ref[...] = either(part, rest[128:], rest[:128])
    next_ref[...] = either(part, rest[:128], rest[128:])


def level1_kernel(own_ref, got_ref, low_ref, low_got_ref, caps_ref, both_ref, send_ref, next_ref):
    _, _, _, y_high = bits()
    own, other = own_ref[...], got_ref[...]
    both = solved(own, other, caps_ref[1])
    both_ref[...] = both
    rest = rest_of(own, other, both, unfolded(low_ref[...])[:, 896:], unfolded(low_got_ref[...])[:, 896:])
    send_ref[:, :448] = either(y_high, rest[64:], rest[:64])
    next_ref[:, :448] = either(y_high, rest[:64], rest[64:])
    send_ref[:, 448:] = jnp.zeros((64, 64), F32)
    next_ref[:, 448:] = jnp.zeros((64, 64), F32)


def level2_kernel(own_ref, got_ref, low_ref, low_got_ref, caps_ref, both_ref, next_ref):
    own, other = own_ref[:, :448], got_ref[:, :448]
    both = solved(own, other, caps_ref[2])
    both_ref[...] = both
    next_ref[...] = rest_of(own, other, both, low_ref[:, 512:896], low_got_ref[:, 512:896])


def level3_kernel(own_ref, got_ref, swap_ref, swap_got_ref, caps_ref, both_ref, next_ref,
                  send_ref):
    _, core, _, _ = bits()
    own, other = own_ref[...], got_ref[...]
    both = solved(own, other, caps_ref[3])
    both_ref[...] = both
    mine, got = swap_ref[...], swap_got_ref[...]
    a, b = either(core, mine, got), either(core, got, mine)
    row_own = side(a[:, :128], b[:, :128], a[:, 256:320])
    row_other = side(a[:, 128:256], b[:, 128:256], a[:, 320:384])
    rest = rest_of(own, other, both, row_own, row_other)
    next_ref[...] = rest
    send_ref[...] = folded(rest)


def level4_kernel(own_ref, got_ref, swap_ref, swap_got_ref, caps_ref, both_ref, next_ref):
    _, core, _, _ = bits()
    own, other = own_ref[...], unfolded(got_ref[...])
    both = solved(own, other, caps_ref[4])
    both_ref[...] = both
    mine, got = unfolded(swap_ref[...]), unfolded(swap_got_ref[...])
    a, b = either(core, mine, got), either(core, got, mine)
    row_own = side(a[:, :128], b[:, :128])
    row_other = side(a[:, 128:256], b[:, 128:256])
    next_ref[...] = rest_of(own, other, both, row_own, row_other)


def level5_kernel(own_ref, got_ref, swap4_ref, swap4_got_ref, swap_ref, swap_got_ref, caps_ref,
                  both0_ref, both_ref, next_ref, down_ref):
    _, core, _, _ = bits()
    down_ref[...] = folded(both0_ref[:, RANK:])
    own, other = own_ref[...], got_ref[...]
    both = solved(own, other, caps_ref[5])
    both_ref[...] = both
    mine, got = unfolded(swap4_ref[...]), unfolded(swap4_got_ref[...])
    a4, b4 = either(core, mine, got), either(core, got, mine)
    mine, got = swap_ref[...], swap_got_ref[...]
    a, b = either(core, mine, got), either(core, got, mine)
    row_own = side(a4[:, 256:320], b4[:, 256:320], b[:, 192:])
    row_other = side(a[:, :64], b[:, :128])
    rest = rest_of(own, other, both, row_own, row_other)
    next_ref[...] = side(rest, a[:, 128:192], b[:, 128:192], a[:, 64:128])


def level6_kernel(own_ref, got_ref, caps_ref, both_ref, next_ref):
    own, other = own_ref[:, :192], got_ref[:, :192]
    both = solved(own, other, caps_ref[6])
    both_ref[...] = both
    rest = rest_of(own, other, both, own_ref[:, 192:320], got_ref[:, 192:320])
    next_ref[...] = folded(side(rest, own_ref[:, 320:] + got_ref[:, 320:]))


def level7_kernel(own_ref, got_ref, caps_ref, both_ref, next_ref):
    mine, theirs = unfolded(own_ref[...]), unfolded(got_ref[...])
    own, other = mine[:, :128], theirs[:, :128]
    both = solved(own, other, caps_ref[7])
    both_ref[...] = both
    next_ref[...] = folded(rest_of(own, other, both, mine[:, 128:], theirs[:, 128:]))


def level8_kernel(own_ref, got_ref, both1_ref, both2_ref, both3_ref, both4_ref, both5_ref,
                  both6_ref, both7_ref, caps_ref, out_ref):
    both = solved(unfolded(own_ref[...]), unfolded(got_ref[...]), caps_ref[8])
    out_ref[:, :128] = side(both3_ref[:, :RANK], both4_ref[:, :RANK])
    out_ref[:, 128:256] = side(both5_ref[:, :RANK], both6_ref[:, :RANK])
    out_ref[:, 256:384] = side(both7_ref[:, :RANK], both[:, :RANK])
    out_ref[:, 384:512] = both2_ref[...]
    out_ref[:, 512:640] = both1_ref[:64, :]
    out_ref[:, 640:] = both1_ref[64:, :]


def place(shard):
    core, part, y_high = shard >> 2, shard >> 1 & 1, shard & 1
    return y_high << 2 | (part ^ y_high) << 1 | core


def final_kernel(theirs_ref, mine_ref, got_ref, both0_ref, all_ref, high_ref, low_ref, out_ref,
                 block_ref, sems):
    _, core, part, y_high = bits()
    halves = []
    for c in range(2):
        rows = []
        for b1 in range(2):
            quad = all_ref[y_high << 2 | (b1 ^ y_high) << 1 | c]
            for b2 in range(2):
                level1 = quad[:, 512 + 128 * b2 : 640 + 128 * b2]
                level1 = either(part ^ b1, level1[:, :RANK], level1[:, RANK:])
                block = all_ref[place(4 * c + 2 * b1 + b2)]
                level2 = either(y_high ^ b2, block[:, 384:448], block[:, 448:512])
                rows.append(side(level1, level2, block[:, :384]))
        halves.append(stack(*rows))
    first, second = halves
    own = split(side(both0_ref[:, :RANK], either(core, first, second)))
    other = split(side(unfolded(got_ref[...], 256), either(core, second, first)))
    copies = []
    for n in range(2):
        rows = slice(256 * n, 256 * (n + 1))
        factors = (high_ref[rows, :], low_ref[rows, :])
        own_out = mine_ref[rows, :] - mm3(factors, own, NT)
        other_out = theirs_ref[rows, :] - mm3(factors, other, NT)
        block_ref[n, :, :256] = either(core, own_out, other_out)
        block_ref[n, :, 256:] = either(core, other_out, own_out)
        copies.append(
            pltpu.make_async_copy(block_ref.at[n], out_ref.at[pl.ds(256 * n, 256)], sems.at[n])
        )
        copies[n].start()
    for copy in copies:
        copy.wait()


def final(*args):
    return pl.pallas_call(
        final_kernel,
        out_shape=jax.ShapeDtypeStruct((512, 512), F32),
        in_specs=[pl.BlockSpec(memory_space=pltpu.VMEM)] * len(args),
        out_specs=pl.BlockSpec(memory_space=pl.ANY),
        scratch_shapes=[pltpu.VMEM((2, 256, 512), F32), pltpu.SemaphoreType.DMA((2,))],
        compiler_params=pltpu.CompilerParams(vmem_limit_bytes=16 * 2**20),
        cost_estimate=pl.CostEstimate(
            flops=12 * 75_000_000, bytes_accessed=2**20, transcendentals=0
        ),
    )(*args)


def local(rhs, leaf_inverse, basis, caps):
    partial = functools.partial
    high, low, gram_send, gram_keep = call(
        gram_kernel, [((576, 512), BF16), ((576, 512), BF16), (256, 512), (256, 512)],
        basis.T, flops=6 * 100_000_000, grant=12,
    )
    gram_got = sent(gram_send, PARTNER[0])
    iterate_theirs, terms_theirs = call(
        partial(solve_kernel, True), [(512, 256), (256, 640)],
        rhs, leaf_inverse, high, low, flops=6 * 142_000_000, grant=12,
    )
    terms_got = sent(terms_theirs, PARTNER[0])
    gram1, = call(gram_core_kernel, [(672, 128)], gram_keep, gram_got, tokens=(terms_theirs,))
    gram1_got = sent(gram1, PARTNER[1])
    iterate_own, terms = call(
        partial(solve_kernel, False), [(512, 256), (256, 640)],
        rhs, leaf_inverse, high, low, tokens=(gram1,), flops=6 * 142_000_000, grant=12,
    )
    caps, = call(caps_kernel, [(9, 128, 128)], caps[0])
    both0, send1, state = call(
        level0_kernel, [(256, 128), (128, 512), (128, 512)],
        terms, terms_got, gram_keep, gram_got, caps,
    )
    got = sent(send1, PARTNER[1])
    gram2, = call(gram_y_kernel, [(64, 896)], gram1, gram1_got, tokens=(send1,))
    gram2_got = sent(gram2, PARTNER[2])
    both1, send2, state = call(
        level1_kernel, [(128, 128), (64, 512), (64, 512)], state, got, gram1, gram1_got, caps
    )
    got = sent(send2, PARTNER[2])
    gram, = call(gram_add_kernel, [(64, 512)], gram2, gram2_got, tokens=(send2,))
    grams = gram, sent(gram, PARTNER[3])
    both2, state = call(
        level2_kernel, [(64, 128), (64, 384)], state, got, gram2, gram2_got, caps
    )
    basis_high, basis_low = call(
        basis_kernel, [((512, 576), BF16), ((512, 576), BF16)], basis.T, tokens=(state,)
    )
    got = sent(state, PARTNER[3])
    swap, gram, going = call(
        partial(gram_level_kernel, 3), GRAM_OUTS[3], *grams, tokens=(state,)
    )
    swap_got = sent(swap, PARTNER[0])
    grams = gram, sent(going, PARTNER[4])
    both3, state, going = call(
        level3_kernel, [(64, 128), (64, 320), (160, 128)], state, got, swap, swap_got, caps
    )
    got = sent(going, PARTNER[4])
    swap4, gram, going = call(
        partial(gram_level_kernel, 4), GRAM_OUTS[4], *grams, tokens=(state,)
    )
    swap4_got = sent(swap4, PARTNER[0])
    grams = gram, sent(going, PARTNER[5])
    both4, state = call(
        level4_kernel, [(64, 128), (64, 256)],
        state, got, swap4, swap4_got, caps, tokens=(basis_low,),
    )
    got = sent(state, PARTNER[5])
    swap, = call(partial(gram_level_kernel, 5), GRAM_OUTS[5], *grams, tokens=(state,))
    swap_got = sent(swap, PARTNER[0])
    both5, state, down = call(
        level5_kernel, [(64, 128), (64, 384), (128, 128)],
        state, got, swap4, swap4_got, swap, swap_got, caps, both0,
    )
    got = sent(state, PARTNER[6])
    down_got = sent(down, PARTNER[0])
    both6, state = call(
        level6_kernel, [(64, 128), (96, 128)], state, got, caps, tokens=(down_got,)
    )
    got = sent(state, PARTNER[7])
    both7, state = call(level7_kernel, [(64, 128), (32, 128)], state, got, caps)
    got = sent(state, PARTNER[8])
    last, = call(
        level8_kernel, [(64, 768)],
        state, got, both1, both2, both3, both4, both5, both6, both7, caps,
    )
    octets = [list(range(n, n + 8)) for n in range(0, 512, 8)]
    gathered = lax.all_gather(last, "leaf", axis_index_groups=octets)
    return final(
        iterate_theirs, iterate_own, down_got, both0, gathered, basis_high, basis_low
    )


def solution(mesh):
    return jax.shard_map(
        local,
        mesh=mesh,
        in_specs=(P("leaf", None), P("leaf", None), P("leaf", None), P("leaf", None, None, None)),
        out_specs=P("leaf", None),
        check_vma=False,
    )
```
